128 devices in a mesh: row: 8 (over x, core), col: 16 (over z, y).
Axes of the slice: x: 4, y: 4, z: 4, core: 2. Of those that a mesh axis runs over, the one named last changes fastest.
Arguments:
- points: float32 [3, 262144], P(None, ('row', 'col')), may hold values from 0 to 1
- targets: float32 [262144], P(('row', 'col')), may hold values from -0.75 to 3.75
- kd_order: int32 [262144], P(('row', 'col')), may hold values from 0 to 2047, as said below
- lengthscales: float32 [8], replicated, may hold values from 0.5 to 2.14, as said below
- noise_level: float32 [8], replicated, may hold values from 2 to 4
- block_owner: int32 [512], replicated, may hold values from 0 to 511, as said below
- block_pairs: int32 [3, 2048], replicated, may hold values from 0 to 511, as said below
Outputs:
- solution: float32 [8, 262144], P(None, ('row', 'col'))
- residual: float32 [8, 262144], P(None, ('row', 'col'))
The draws below stay inside these ranges and needn't reach their ends.
Inputs may be any that keep to these rules, and one draw needn't show every extreme that they name: `kd_order`: each device's 2048 entries are a permutation of 0 to 2047. `block_owner`: A permutation: the slot of each block id; slot s is local block s % 4 of device s // 4. `block_pairs`: rows 0 and 1 are block ids, row 2 a lengthscale index below 8. Columns 16 d to 16 d + 15 are device d's pairs: the first block's slot lies on device d, the second block's on another device with the same row index. At most 2 of one device's pairs have their second block on one device, and exactly 2 on some device, for every device. `lengthscales`: Ascending.
All inputs are finite; a program needn't handle non-finite values.
Results may differ from the reference program's by a relative error of at most 0.00071.
Values may be sent and summed in bfloat16 or wider, within the bound.
No kernel may reach another device: no remote copies, remote signals or barrier semaphores. Data moves between devices by JAX's collectives and lax.ppermute only.
A program may use at most 256 MiB of HBM per device.

```python
import math
import jax
import jax.numpy as jnp
from jax import lax

BLOCK = 512
LS = 8
CAP = 2
B_DEV = 4
PAIRS = 16
PTS_DEV = 2048
NBLK = 512
NPTS = 262144
N_ROW = 8
N_COL = 16


def owner_table(key):
    return jax.random.permutation(jax.random.fold_in(key, 101), NBLK).astype(jnp.int32)


def draw_block_owner(key, part):
    table = owner_table(key)
    return table


def draw_block_pairs(key, part):
    table = owner_table(key)
    key = jax.random.fold_in(key, 6)
    devices = N_ROW * N_COL
    holder = jnp.argsort(table, stable=True).astype(jnp.int32)
    pool_size = (N_COL - 1) * CAP

    def device_pairs(device):
        device_key = jax.random.fold_in(key, device)
        streams = jax.random.split(device_key, 6)
        row_index = device // N_COL
        col_index = device % N_COL
        others = (col_index + 1 + jnp.arange(N_COL - 1)) % N_COL
        full_peer = jax.random.randint(streams[0], (), 0, N_COL - 1)
        pool_slots = jnp.arange(pool_size)
        scores = jax.random.permutation(streams[1], pool_size) + jnp.where(pool_slots // CAP == full_peer, pool_size, 0)
        taken = jnp.argsort(scores, stable=True)[:PAIRS - CAP] // CAP
        chosen = jnp.concatenate([jnp.full((CAP,), full_peer, jnp.int32), taken.astype(jnp.int32)])
        chosen = chosen[jax.random.permutation(streams[2], PAIRS)]
        partner_col = others[chosen]
        first_local = jax.random.randint(streams[3], (PAIRS,), 0, B_DEV)
        second_local = jax.random.randint(streams[4], (PAIRS,), 0, B_DEV)
        reach = jax.random.randint(streams[5], (PAIRS,), 0, LS)
        first_block = holder[device * B_DEV + first_local]
        second_block = holder[(row_index * N_COL + partner_col) * B_DEV + second_local]
        return jnp.stack([first_block, second_block, reach.astype(jnp.int32)])
    listed = jax.vmap(device_pairs)(jnp.arange(devices))
    return jnp.transpose(listed, (1, 0, 2)).reshape(3, devices * PAIRS).astype(jnp.int32)


def draw_kd_order(key, part):
    key = jax.random.fold_in(key, 3)
    devices = N_ROW * N_COL
    streams = jax.random.split(key, devices)

    def shuffled(stream):
        return jax.random.permutation(stream, PTS_DEV)
    return jax.vmap(shuffled)(streams).reshape(NPTS).astype(jnp.int32)


def draw_targets(key, part):
    key = jax.random.fold_in(key, 4)
    devices = N_ROW * N_COL
    device = (jnp.arange(NPTS) // PTS_DEV).astype(jnp.float32)
    growth = jnp.exp(device / max(devices - 1, 1) * jnp.log(3.0))
    base = jax.random.uniform(key, (NPTS,), jnp.float32, -0.25, 1.25)
    return base * growth


def draw_lengthscales(key, part):
    key = jax.random.fold_in(key, 5)
    jitter = jax.random.uniform(key, (LS,), jnp.float32, 1.0, 1.19)
    return 0.5 * jnp.exp(jnp.arange(LS).astype(jnp.float32) * jnp.log(1.2)) * jitter


def block_scale(rng, dims, shards, smallest, top_value):
    gain, own = 1.0, jax.random.fold_in(rng, 6)
    for position, blocks in shards:
        steps = jnp.exp(jax.random.uniform(jax.random.fold_in(own, position), (blocks,), jnp.float32, smallest / len(shards), top_value / len(shards)))
        gain = gain * jnp.repeat(steps, dims[position] // blocks).reshape([-1 if axis == position else 1 for axis in range(len(dims))])
    return gain


def setup_inputs(seed: int = 0) -> dict:
    key_list = jax.random.split(jax.random.key(seed), 8)
    points = jnp.clip(1.0 * jax.random.uniform(key_list[0], (3, NPTS), jnp.float32) ** block_scale(key_list[0], (3, NPTS), ((1, 128),), -0.2, 0.2), 0.0, 1.0)
    targets = draw_targets(jax.random.fold_in(key_list[7], 71), 0)
    kd_order = draw_kd_order(jax.random.fold_in(key_list[7], 71), 0)
    lengthscales = draw_lengthscales(jax.random.fold_in(key_list[7], 71), 0)
    noise_level = jnp.clip(jnp.exp(jax.random.uniform(key_list[4], (LS,), jnp.float32, math.log(2.0), math.log(4.0))), 2.0, 4.0)
    block_owner = draw_block_owner(jax.random.fold_in(key_list[7], 71), 0)
    block_pairs = draw_block_pairs(jax.random.fold_in(key_list[7], 71), 0)
    return {"points": points, "targets": targets, "kd_order": kd_order, "lengthscales": lengthscales, "noise_level": noise_level, "block_owner": block_owner, "block_pairs": block_pairs}


def squared_gap(first_pts, second_pts):
    summed = jnp.zeros((first_pts.shape[1], second_pts.shape[1]), jnp.float32)
    for component in range(3):
        differ = first_pts[component][:, None] - second_pts[component][None, :]
        summed = summed + differ * differ
    return summed

def wendland(squared, scales):
    radius = jnp.sqrt(squared)[None, :, :] / scales[:, None, None]
    remain = jnp.maximum(1.0 - radius, 0.0)
    return (remain * remain * remain * remain * (4.0 * radius + 1.0)).astype(jnp.bfloat16)

def apply_operator(vector, blocked, first_slot, second_slot, live_mask, scales, noise_level):
    rounded = vector.astype(jnp.bfloat16)

    def own_part(inputs):
        kernel = wendland(squared_gap(inputs[0], inputs[0]), scales).astype(jnp.float32)
        return jnp.einsum('lij,lj->li', kernel, inputs[1].astype(jnp.float32))

    def cross_part(inputs):
        kernel = wendland(squared_gap(blocked[inputs[0]], blocked[inputs[1]]), scales).astype(jnp.float32)
        forward = jnp.einsum('lij,lj->li', kernel, rounded[inputs[1]].astype(jnp.float32)) * inputs[2][:, None]
        backward = jnp.einsum('lij,li->lj', kernel, rounded[inputs[0]].astype(jnp.float32)) * inputs[2][:, None]
        return (forward, backward)
    summed = lax.map(own_part, (blocked, rounded), batch_size=16)
    forward, backward = lax.map(cross_part, (first_slot, second_slot, live_mask), batch_size=16)
    summed = summed.at[first_slot].add(forward).at[second_slot].add(backward)
    return noise_level[None, :, None] * vector + summed / (2.0 * BLOCK)

def to_points(field):
    return jnp.transpose(field, (1, 0, 2)).reshape(LS, NPTS)

def reference(points, targets, kd_order, lengthscales, noise_level, block_owner, block_pairs):
    offsets = jnp.arange(NPTS) // PTS_DEV * PTS_DEV
    gather_at = (kd_order + offsets).astype(jnp.int32)
    blocked = jnp.transpose(points[:, gather_at].reshape(3, NBLK, BLOCK), (1, 0, 2))
    right_side = targets[gather_at].reshape(NBLK, 1, BLOCK)
    first_slot = block_owner[block_pairs[0]].astype(jnp.int32)
    second_slot = block_owner[block_pairs[1]].astype(jnp.int32)
    live_mask = (jnp.arange(LS)[None, :] >= block_pairs[2][:, None]).astype(jnp.float32)
    residual = jnp.broadcast_to(right_side, (NBLK, LS, BLOCK)).astype(jnp.float32)
    solution = jnp.zeros((NBLK, LS, BLOCK), jnp.float32)
    direction = residual
    norm_now = lax.optimization_barrier(jnp.sum(residual * residual, axis=(0, 2)))
    for iteration in range(2):
        mapped = apply_operator(direction, blocked, first_slot, second_slot, live_mask, lengthscales, noise_level)
        step_size = norm_now / lax.optimization_barrier(jnp.sum(direction * mapped, axis=(0, 2)))
        solution = solution + step_size[None, :, None] * direction
        residual = residual - step_size[None, :, None] * mapped
        if iteration == 0:
            norm_next = lax.optimization_barrier(jnp.sum(residual * residual, axis=(0, 2)))
            direction = residual + (norm_next / norm_now)[None, :, None] * direction
            norm_now = norm_next
    return (to_points(solution), to_points(residual))
```

```python
import jax
import jax.numpy as jnp
from jax import lax
from jax.experimental import pallas as pl
from jax.experimental.pallas import tpu as pltpu
from jax.sharding import PartitionSpec as P

BLOCK = 512
LS = 8
CAP = 2
LANES = 128
CHUNK = 16
F32 = jnp.float32
BF16 = jnp.bfloat16
VMEM = pltpu.VMEM
SMEM = pltpu.SMEM
LIMIT = 56 * 2**20


def vmem_spec():
    return pl.BlockSpec(memory_space=pltpu.VMEM)


def smem_spec():
    return pl.BlockSpec(memory_space=pltpu.SMEM)


def any_spec():
    return pl.BlockSpec(memory_space=pl.ANY)


def params():
    return pltpu.CompilerParams(vmem_limit_bytes=LIMIT)


def prepare_kernel(
    cols, count, pairs_dev, me_ref, pts_ref, tgt_ref, order_ref, owner_ref, pairs_ref,
    loc_ref, send_ref, meta_ref, asked_ref, used_ref,
):
    me = me_ref[0]
    row = me // cols

    def clear(i, _):
        asked_ref[i] = -1
        return 0

    lax.fori_loop(0, cols * CAP + 1, clear, 0)
    for c in range(cols):
        used_ref[c] = 0

    def own_pair(p, _):
        column = me * pairs_dev + p
        first = owner_ref[pairs_ref[0, column]]
        second = owner_ref[pairs_ref[1, column]]
        partner = (second // count) % cols
        seen = used_ref[partner]
        used_ref[partner] = seen + 1
        meta_ref[0, p] = first % count
        meta_ref[1, p] = partner * CAP + seen
        meta_ref[2, p] = pairs_ref[2, column]
        return 0

    lax.fori_loop(0, pairs_dev, own_pair, 0)

    def scan_source(c, _):
        base = (row * cols + c) * pairs_dev
        seen = jnp.int32(0)
        for j in range(pairs_dev):
            second = owner_ref[pairs_ref[1, base + j]]
            match = (second // count) == me
            place = jnp.where(match, c * CAP + seen, cols * CAP)
            asked_ref[place] = second % count
            seen = seen + match.astype(jnp.int32)
        return 0

    lax.fori_loop(0, cols, scan_source, 0)

    total = pts_ref.shape[1]
    pieces = total // LANES
    source = jnp.concatenate([pts_ref[...], tgt_ref[...], jnp.zeros((4, total), F32)], axis=0)
    for o in range(pieces):
        index = jnp.broadcast_to(order_ref[:, o * LANES:(o + 1) * LANES], (8, LANES))
        high = index // LANES
        low = index % LANES
        got = jnp.zeros((8, LANES), F32)
        for c in range(pieces):
            part = jnp.take_along_axis(
                source[:, c * LANES:(c + 1) * LANES], low, axis=1, mode="promise_in_bounds"
            )
            got = jnp.where(high == c, part, got)
        per = BLOCK // LANES
        loc_ref[o // per, :, (o % per) * LANES:(o % per + 1) * LANES] = got

    for q in range(cols * CAP):
        meta_ref[3, q] = asked_ref[q]
        where = jnp.maximum(asked_ref[q], 0)
        half = (q % CAP) * 4
        send_ref[q // CAP, half:half + 4, :] = loc_ref[where, 0:4, :]


def spread_columns(rows):
    turned = jnp.transpose(rows)
    return [jnp.broadcast_to(turned[:, k:k + 1], (BLOCK, LANES)) for k in range(8)]


def rounded(values):
    return values.astype(BF16).astype(F32)


def per_system(ref):
    which = lax.broadcasted_iota(jnp.int32, (LS, LANES), 0)
    out = jnp.zeros((LS, LANES), F32)
    for l in range(LS):
        out = jnp.where(which == l, ref[l], out)
    return out


def wide(column, width):
    return jnp.concatenate([column] * (width // LANES), axis=1)


def lane_fold(values):
    total = values[:, 0:LANES]
    for c in range(1, values.shape[1] // LANES):
        total = total + values[:, c * LANES:(c + 1) * LANES]
    return total


def distance(col_refs, row_vals, width):
    summed = None
    for k in range(3):
        differ = wide(col_refs[k], width) - row_vals[k]
        square = differ * differ
        summed = square if summed is None else summed + square
    summed = jnp.maximum(summed, 1e-30)
    return summed * lax.rsqrt(summed)


CREST = 4.0**0.2


def kernel_value(dist, slope):
    remain = jnp.maximum(CREST - dist * slope, 0.0)
    squared = remain * remain
    return ((squared * squared) * (5.0 / CREST**4 - remain)).astype(BF16)


def sub_fold(values):
    return values[0:8, :] + values[8:16, :]


def fold_forward(forward_ref, s):
    lane = lax.broadcasted_iota(jnp.int32, (LANES, LANES), 1)
    out = []
    for part in range(BLOCK // LANES):
        held = jnp.zeros((LANES, LANES), F32)
        for l in range(LS):
            block = forward_ref[s, l, part * LANES:(part + 1) * LANES, :]
            held = jnp.where(lane == l, jnp.sum(block, axis=1, keepdims=True), held)
        out.append(jnp.transpose(held)[0:LS, :])
    return jnp.concatenate(out, axis=1)


def own_kernel(common, ls_ref, loc_ref, vec_ref, out_ref, coord_ref, col_ref, dist_ref, forward_ref):
    count = loc_ref.shape[0]
    parts = BLOCK // LANES
    per = LANES // CHUNK

    def block(s, _):
        columns = spread_columns(loc_ref[s])
        for k in range(4):
            coord_ref[k] = columns[k]
        if common:
            coord_ref[3] = rounded(columns[3])
        else:
            columns = spread_columns(vec_ref[s])
            for l in range(LS):
                col_ref[l] = columns[l]
        for part in range(parts):
            low = part * LANES
            width = BLOCK - low
            rows = [loc_ref[s, k:k + 1, low:] for k in range(3)]

            def measure(c, _):
                at = pl.ds(pl.multiple_of(low + c * CHUNK, CHUNK), CHUNK)
                dist_ref[at, low:] = distance([coord_ref[k, at, :] for k in range(3)], rows, width)
                return 0

            lax.fori_loop(0, per, measure, 0, unroll=2)

        def two(t, _):
            back = [jnp.zeros((8, BLOCK), F32) for _ in range(2)]
            ids = [2 * t, 2 * t + 1]
            slopes = [ls_ref[l] for l in ids]
            for part in range(parts):
                low = part * LANES
                width = BLOCK - low
                if common:
                    rows = [rounded(loc_ref[s, 3:4, low:])] * 2
                else:
                    rows = [vec_ref[s, pl.ds(l, 1), :][:, low:] for l in ids]

                def step(c, held):
                    at = pl.ds(pl.multiple_of(low + c * CHUNK, CHUNK), CHUNK)
                    dist = dist_ref[at, low:]
                    fresh = []
                    for n in range(2):
                        value = kernel_value(dist, slopes[n]).astype(F32)
                        forward_ref[s, ids[n], at, :] = lane_fold(value * rows[n])
                        if width > LANES:
                            column = coord_ref[3, at, :] if common else col_ref[ids[n], at, :]
                            right = value[:, LANES:] * wide(column, width - LANES)
                            fresh.append(held[n] + sub_fold(right))
                    return tuple(fresh) if fresh else held

                start = max(width - LANES, LANES)
                held = tuple(jnp.zeros((8, start), F32) for _ in range(2))
                held = lax.fori_loop(0, per, step, held, unroll=2)
                if width > LANES:
                    for n in range(2):
                        back[n] = jnp.concatenate(
                            [back[n][:, :low + LANES], back[n][:, low + LANES:] + held[n]], axis=1
                        )
            for n in range(2):
                out_ref[s, pl.ds(ids[n], 1), :] = jnp.sum(back[n], axis=0, keepdims=True)
            return 0

        lax.fori_loop(0, LS // 2, two, 0)
        out_ref[s] = out_ref[s] + fold_forward(forward_ref, s)
        return 0

    lax.fori_loop(0, count, block, 0)


def first_kernel(
    ls_ref, meta_ref, loc_ref, far_ref,
    out_ref, back_ref, tiles_ref,
    coord_ref, dist_ref, forward_ref, stage_ref, sem_ref,
):
    count = loc_ref.shape[0]
    pairs_dev = tiles_ref.shape[0] // LS
    steps = BLOCK // CHUNK
    for s in range(count):
        columns = spread_columns(loc_ref[s])
        for k in range(3):
            coord_ref[s, k] = columns[k]
        coord_ref[s, 3] = rounded(columns[3])
    forward_ref[...] = jnp.zeros(forward_ref.shape, F32)

    def store_copy(slot, number):
        return pltpu.make_async_copy(stage_ref.at[slot], tiles_ref.at[number], sem_ref.at[slot])

    def pair(p, number):
        a = meta_ref[0, p]
        q = meta_ref[1, p]
        reach = meta_ref[2, p]
        both = far_ref[q // CAP]
        mine = jnp.where(q % CAP == 1, both[4:8, :], both[0:4, :])
        rows = [mine[k:k + 1, :] for k in range(3)]
        values = rounded(mine[3:4, :])

        def measure(c, _):
            at = pl.ds(pl.multiple_of(c * CHUNK, CHUNK), CHUNK)
            dist_ref[at, :] = distance([coord_ref[a, k, at, :] for k in range(3)], rows, BLOCK)
            return 0

        lax.fori_loop(0, steps, measure, 0, unroll=2)
        back_ref[q] = jnp.zeros((LS, BLOCK), F32)

        def sweep(ids, number):
            slopes = [ls_ref[l] for l in ids]
            slots = [(number + n) % 4 for n in range(len(ids))]
            for n in range(len(ids)):
                @pl.when(number + n >= 4)
                def _():
                    store_copy(slots[n], number + n).wait()

            def step(c, held):
                at = pl.ds(pl.multiple_of(c * CHUNK, CHUNK), CHUNK)
                dist = dist_ref[at, :]
                column = wide(coord_ref[a, 3, at, :], BLOCK)
                fresh = []
                for n in range(len(ids)):
                    value = kernel_value(dist, slopes[n])
                    stage_ref[slots[n], at, :] = value
                    value = value.astype(F32)
                    forward_ref[a, ids[n], at, :] += lane_fold(value * values)
                    fresh.append(held[n] + sub_fold(value * column))
                return tuple(fresh)

            held = tuple(jnp.zeros((8, BLOCK), F32) for _ in ids)
            held = lax.fori_loop(0, steps, step, held, unroll=2)
            for n in range(len(ids)):
                back_ref[q, pl.ds(ids[n], 1), :] = jnp.sum(held[n], axis=0, keepdims=True)
                store_copy(slots[n], number + n).start()
            return number + len(ids)

        live = LS - reach

        def two(t, number):
            return sweep([LS - 1 - 2 * t, LS - 2 - 2 * t], number)

        number = lax.fori_loop(0, live // 2, two, number)
        return lax.cond(live % 2 == 1, lambda m: sweep([reach], m), lambda m: m, number)

    number = lax.fori_loop(0, pairs_dev, pair, jnp.int32(0))
    for back in range(4):
        store_copy((number - 1 - back) % 4, number - 1 - back).wait()
    for s in range(count):
        out_ref[s] = fold_forward(forward_ref, s)


def combine_kernel(
    meta_ref, loc_ref, own_ref, fwd_ref, got_ref, w_ref, send_ref, dots_ref
):
    count = loc_ref.shape[0]
    slots = got_ref.shape[0]
    w_ref[...] = own_ref[...] + fwd_ref[...]
    for q in range(slots):
        where = meta_ref[3, q]

        @pl.when(where >= 0)
        def _():
            w_ref[where] = w_ref[where] + got_ref[q]

    unit = 1.0 / (2.0 * BLOCK)
    products = [jnp.zeros((LS, BLOCK), F32) for _ in range(3)]
    for s in range(count):
        value = w_ref[s] * unit
        w_ref[s] = value
        target = jnp.broadcast_to(loc_ref[s, 3:4, :], (LS, BLOCK))
        products[0] = products[0] + target * target
        products[1] = products[1] + target * value
        products[2] = products[2] + value * value
    for q in range(slots):
        send_ref[q] = w_ref[jnp.maximum(meta_ref[3, q], 0)]
    lane = lax.broadcasted_iota(jnp.int32, (LS, LANES), 1)
    held = jnp.zeros((LS, LANES), F32)
    for n in range(3):
        held = jnp.where(lane == n, jnp.sum(products[n], axis=1, keepdims=True), held)
    dots_ref[...] = held


def second_kernel(
    meta_ref, loc_ref, w_ref, own_ref, far_pts_ref, far_ref, dots_ref, tiles_ref,
    out_ref, back_ref,
    list_ref, col_ref, forward_ref, wz_ref, yz_ref, stage_ref, sem_ref,
):
    count = w_ref.shape[0]
    pairs_dev = tiles_ref.shape[0] // LS
    steps = BLOCK // CHUNK
    depth = stage_ref.shape[0]

    def list_pair(p, number):
        reach = meta_ref[2, p]
        live = LS - reach

        def two(t, number):
            list_ref[number] = p * LS + LS - 1 - t
            return number + 1

        return lax.fori_loop(0, live, two, number)

    number = lax.fori_loop(0, pairs_dev, list_pair, jnp.int32(0))

    def load_copy(t):
        slot = t % depth
        return pltpu.make_async_copy(tiles_ref.at[t], stage_ref.at[slot], sem_ref.at[slot])

    for t in range(depth - 1):
        load_copy(jnp.int32(t)).start()

    def clear(p, _):
        q = meta_ref[1, p]
        back_ref[q // CAP, pl.ds(pl.multiple_of((q % CAP) * LS, LS), LS), :] = jnp.zeros((LS, BLOCK), F32)
        return 0

    lax.fori_loop(0, pairs_dev, clear, 0)
    for s in range(count):
        columns = spread_columns(w_ref[s])
        for l in range(LS):
            col_ref[s, l] = columns[l]
    forward_ref[...] = jnp.zeros(forward_ref.shape, F32)
    wz_ref[...] = jnp.zeros(wz_ref.shape, F32)
    yz_ref[...] = jnp.zeros(yz_ref.shape, F32)

    def tile(t, _):
        entry = list_ref[t]
        p = entry // LS
        l = entry % LS
        a = meta_ref[0, p]
        q = meta_ref[1, p]
        slot = t % depth

        @pl.when(t + depth - 1 < number)
        def _():
            load_copy(t + depth - 1).start()

        load_copy(t).wait()
        row = far_ref[q, pl.ds(l, 1), :]

        def step(c, held):
            at = pl.ds(pl.multiple_of(c * CHUNK, CHUNK), CHUNK)
            value = stage_ref[slot, at, :].astype(F32)
            forward_ref[a, l, at, :] += lane_fold(value * row)
            return held + sub_fold(value * wide(col_ref[a, l, at, :], BLOCK))

        held = lax.fori_loop(0, steps, step, jnp.zeros((8, BLOCK), F32), unroll=4)
        result = jnp.sum(held, axis=0, keepdims=True)
        back_ref[q // CAP, pl.ds((q % CAP) * LS + l, 1), :] = result
        both = far_pts_ref[q // CAP]
        target = jnp.where(q % CAP == 1, both[7:8, :], both[3:4, :])
        wz_ref[pl.ds(l, 1), :] += result * row
        yz_ref[pl.ds(l, 1), :] += result * target
        return 0

    lax.fori_loop(0, number, tile, 0)
    wz = wz_ref[...]
    yz = yz_ref[...]
    for s in range(count):
        value = own_ref[s] + fold_forward(forward_ref, s)
        out_ref[s] = value
        wz = wz + value * w_ref[s]
        yz = yz + value * loc_ref[s, 3:4, :]
    unit = 1.0 / (2.0 * BLOCK)
    lane = lax.broadcasted_iota(jnp.int32, (LS, LANES), 1)
    held = jnp.where(lane == 3, jnp.sum(wz, axis=1, keepdims=True) * unit, dots_ref[...])
    held = jnp.where(lane == 4, jnp.sum(yz, axis=1, keepdims=True) * unit, held)
    padded = jnp.concatenate([held, jnp.zeros((LS, BLOCK - LANES), F32)], axis=1)
    for c in range(back_ref.shape[0]):
        back_ref[c, CAP * LS:(CAP + 1) * LS, :] = padded


def gather_kernel(meta_ref, part_ref, got_ref, z_ref, dots_ref):
    z_ref[...] = part_ref[...]
    held = jnp.zeros((LS, LANES), F32)
    for c in range(got_ref.shape[0]):
        held = held + got_ref[c, CAP * LS:(CAP + 1) * LS, 0:LANES]
        for k in range(CAP):
            where = meta_ref[3, c * CAP + k]

            @pl.when(where >= 0)
            def _():
                z_ref[where] = z_ref[where] + got_ref[c, k * LS:(k + 1) * LS, :]

    z_ref[...] = z_ref[...] * (1.0 / (2.0 * BLOCK))
    for c in range(dots_ref.shape[0]):
        dots_ref[c] = held


def finish_kernel(noise_ref, loc_ref, w_ref, z_ref, dots_ref, sol_ref, res_ref):
    dots = dots_ref[0]
    for c in range(1, dots_ref.shape[0]):
        dots = dots + dots_ref[c]
    noise = per_system(noise_ref)[:, 0:1]
    yy, yw, ww, wz, yz = [dots[:, n:n + 1] for n in range(5)]
    curve = noise * yy + yw
    first = yy / curve
    keep = yw / curve
    fresh = first * ((yy * ww - yw * yw) / curve)
    beta = fresh / yy
    gain = keep + beta
    bend = noise * fresh * (1.0 + beta) + gain * gain * yw - gain * first * (ww + yz) + first * first * wz
    second = fresh / bend
    sol_y = first + second * gain
    sol_w = second * first
    res_y = keep - second * noise * gain
    res_w = second * (noise * first - gain) - first
    for s in range(loc_ref.shape[0]):
        target = loc_ref[s, 3:4, :]
        value = w_ref[s]
        sol_ref[:, s * BLOCK:(s + 1) * BLOCK] = sol_y * target - sol_w * value
        res_ref[:, s * BLOCK:(s + 1) * BLOCK] = res_y * target + res_w * value + sol_w * z_ref[s]


def on_device(points, targets, kd_order, lengthscales, noise_level, block_owner, block_pairs):
    cols = lax.axis_size("col")
    rows = lax.axis_size("row")
    me = (lax.axis_index("row") * cols + lax.axis_index("col")).astype(jnp.int32).reshape(1)
    total = points.shape[1]
    count = total // BLOCK
    pairs_dev = block_pairs.shape[1] // (rows * cols)
    slots = cols * CAP
    field = jax.ShapeDtypeStruct((count, LS, BLOCK), F32)

    loc, send, meta = pl.pallas_call(
        lambda *refs: prepare_kernel(cols, count, pairs_dev, *refs),
        out_shape=(
            jax.ShapeDtypeStruct((count, 8, BLOCK), F32),
            jax.ShapeDtypeStruct((cols, CAP * 4, BLOCK), F32),
            jax.ShapeDtypeStruct((4, slots), jnp.int32),
        ),
        in_specs=[smem_spec(), vmem_spec(), vmem_spec(), vmem_spec(), smem_spec(), smem_spec()],
        out_specs=(vmem_spec(), vmem_spec(), smem_spec()),
        scratch_shapes=[SMEM((slots + 1,), jnp.int32), SMEM((cols,), jnp.int32)],
        compiler_params=params(),
        name="prepare",
    )(me, points, targets.reshape(1, total), kd_order.reshape(1, total), block_owner, block_pairs)

    slopes = CREST / lengthscales

    def own(vec, common):
        return pl.pallas_call(
            lambda *refs: own_kernel(common, *refs),
            out_shape=field,
            in_specs=[smem_spec(), vmem_spec(), vmem_spec()],
            out_specs=vmem_spec(),
            scratch_shapes=[
                VMEM((4, BLOCK, LANES), F32),
                VMEM((LS, BLOCK, LANES), F32),
                VMEM((BLOCK, BLOCK), F32),
                VMEM((count, LS, BLOCK, LANES), F32),
            ],
            compiler_params=params(),
            cost_estimate=pl.CostEstimate(flops=2 * 10**9, bytes_accessed=10**6, transcendentals=0),
            name="own_first" if common else "own_second",
        )(slopes, loc, vec)

    far = lax.all_to_all(send, "col", split_axis=0, concat_axis=0, tiled=True)
    own_one = own(loc, True)
    fwd_one, back_one, tiles = pl.pallas_call(
        first_kernel,
        out_shape=(
            field,
            jax.ShapeDtypeStruct((slots, LS, BLOCK), F32),
            jax.ShapeDtypeStruct((pairs_dev * LS, BLOCK, BLOCK), BF16),
        ),
        in_specs=[smem_spec(), smem_spec(), vmem_spec(), vmem_spec()],
        out_specs=(vmem_spec(), vmem_spec(), any_spec()),
        scratch_shapes=[
            VMEM((count, 4, BLOCK, LANES), F32),
            VMEM((BLOCK, BLOCK), F32),
            VMEM((count, LS, BLOCK, LANES), F32),
            VMEM((4, BLOCK, BLOCK), BF16),
            pltpu.SemaphoreType.DMA((4,)),
        ],
        compiler_params=params(),
        cost_estimate=pl.CostEstimate(flops=10**10, bytes_accessed=6 * 10**7, transcendentals=0),
        name="cross_first",
    )(slopes, meta, loc, far)
    got_one = lax.all_to_all(back_one, "col", split_axis=0, concat_axis=0, tiled=True)

    w, send_w, dots_one = pl.pallas_call(
        combine_kernel,
        out_shape=(
            field,
            jax.ShapeDtypeStruct((slots, LS, BLOCK), F32),
            jax.ShapeDtypeStruct((LS, LANES), F32),
        ),
        in_specs=[smem_spec()] + [vmem_spec()] * 4,
        out_specs=(vmem_spec(),) * 3,
        compiler_params=params(),
        name="combine",
    )(meta, loc, own_one, fwd_one, got_one)
    far_w = lax.all_to_all(send_w, "col", split_axis=0, concat_axis=0, tiled=True)
    own_two = own(w, False)
    fwd_two, back_two = pl.pallas_call(
        second_kernel,
        out_shape=(field, jax.ShapeDtypeStruct((cols, (CAP + 1) * LS, BLOCK), F32)),
        in_specs=[smem_spec()] + [vmem_spec()] * 6 + [any_spec()],
        out_specs=(vmem_spec(),) * 2,
        scratch_shapes=[
            SMEM((pairs_dev * LS,), jnp.int32),
            VMEM((count, LS, BLOCK, LANES), F32),
            VMEM((count, LS, BLOCK, LANES), F32),
            VMEM((LS, BLOCK), F32),
            VMEM((LS, BLOCK), F32),
            VMEM((8, BLOCK, BLOCK), BF16),
            pltpu.SemaphoreType.DMA((8,)),
        ],
        compiler_params=params(),
        cost_estimate=pl.CostEstimate(flops=5 * 10**9, bytes_accessed=6 * 10**7, transcendentals=0),
        name="cross_second",
    )(meta, loc, w, own_two, far, far_w, dots_one, tiles)
    got_two = lax.all_to_all(back_two, "col", split_axis=0, concat_axis=0, tiled=True)

    z, dots_two = pl.pallas_call(
        gather_kernel,
        out_shape=(field, jax.ShapeDtypeStruct((rows, LS, LANES), F32)),
        in_specs=[smem_spec()] + [vmem_spec()] * 2,
        out_specs=(vmem_spec(),) * 2,
        compiler_params=params(),
        name="gather",
    )(meta, fwd_two, got_two)
    dots = lax.all_to_all(dots_two, "row", split_axis=0, concat_axis=0, tiled=True)
    return pl.pallas_call(
        finish_kernel,
        out_shape=(jax.ShapeDtypeStruct((LS, total), F32),) * 2,
        in_specs=[smem_spec()] + [vmem_spec()] * 4,
        out_specs=(vmem_spec(),) * 2,
        compiler_params=params(),
        name="finish",
    )(noise_level, loc, w, z, dots)


def solution(mesh):
    placed = (P(None, ("row", "col")), P(("row", "col")), P(("row", "col")), P(), P(), P(), P())
    return jax.shard_map(
        on_device,
        mesh=mesh,
        in_specs=placed,
        out_specs=(P(None, ("row", "col")), P(None, ("row", "col"))),
        check_vma=False,
    )
```

```python
import jax
import jax.numpy as jnp
from jax import lax
from jax.experimental import pallas as pl
from jax.experimental.pallas import tpu as pltpu
from jax.sharding import PartitionSpec as P

BLOCK = 512
LS = 8
CAP = 2
LANES = 128
CHUNK = 16
DOTS = 5
F32 = jnp.float32
BF16 = jnp.bfloat16
VMEM = pltpu.VMEM
SMEM = pltpu.SMEM
LIMIT = 56 * 2**20


def vmem_spec():
    return pl.BlockSpec(memory_space=pltpu.VMEM)


def smem_spec():
    return pl.BlockSpec(memory_space=pltpu.SMEM)


def any_spec():
    return pl.BlockSpec(memory_space=pl.ANY)


def params():
    return pltpu.CompilerParams(vmem_limit_bytes=LIMIT)


def over(value, size):
    return value >> (size.bit_length() - 1) if size & (size - 1) == 0 else value // size


def rest(value, size):
    return value & (size - 1) if size & (size - 1) == 0 else value % size


def order_kernel(pts_ref, tgt_ref, order_ref, loc_ref, send_ref):
    total = pts_ref.shape[1]
    pieces = total // LANES
    per = BLOCK // LANES
    source = jnp.concatenate([pts_ref[...], tgt_ref[...], jnp.zeros((4, total), F32)], axis=0)
    for o in range(pieces):
        index = jnp.broadcast_to(order_ref[:, o * LANES:(o + 1) * LANES], (8, LANES))
        high = over(index, LANES)
        low = rest(index, LANES)
        got = jnp.zeros((8, LANES), F32)
        for c in range(pieces):
            part = jnp.take_along_axis(
                source[:, c * LANES:(c + 1) * LANES], low, axis=1, mode="promise_in_bounds"
            )
            got = jnp.where(high == c, part, got)
        loc_ref[o // per, :, (o % per) * LANES:(o % per + 1) * LANES] = got
    halves = []
    for h in range(loc_ref.shape[0] // 2):
        halves.append(jnp.concatenate([loc_ref[2 * h, 0:4, :], loc_ref[2 * h + 1, 0:4, :]], axis=0))
    for c in range(send_ref.shape[0] // len(halves)):
        for h in range(len(halves)):
            send_ref[c * len(halves) + h] = halves[h]


SPARE = 63


def plan_kernel(cols, count, pairs_dev, me_ref, owner_ref, pairs_ref, meta_ref, near_ref, far_ref, peer_ref, reach_ref, turn_ref, load_ref, have_ref, used_ref):
    row = over(me_ref[0], cols)
    mine = rest(me_ref[0], cols)
    start = row * (cols * pairs_dev)

    def clear(i, _):
        for c in range(cols):
            have_ref[i * cols + c] = 0
            used_ref[i * cols + c] = 0
        return 0

    lax.fori_loop(0, cols, clear, 0)
    for q in range(cols * CAP):
        meta_ref[4, q] = -1

    def cost_of(reach):
        return 4 * (LS - reach) + 3

    def read(d, _):
        total = jnp.int32(0)
        for j in range(pairs_dev):
            p = d * pairs_dev + j
            first = owner_ref[pairs_ref[0, start + p]]
            second = owner_ref[pairs_ref[1, start + p]]
            reach = pairs_ref[2, start + p]
            e = rest(over(second, count), cols)
            near_ref[p] = rest(first, count)
            far_ref[p] = rest(second, count)
            peer_ref[p] = e
            reach_ref[p] = reach
            total = total + cost_of(reach)
            have_ref[d * cols + e] = have_ref[d * cols + e] + 1
        load_ref[d] = total
        return 0

    lax.fori_loop(0, cols, read, 0)

    def weigh(j, _):
        for d in range(cols):
            p = d * pairs_dev + j
            e = peer_ref[p]
            cost = cost_of(reach_ref[p])
            here = load_ref[d]
            there = load_ref[e]
            back = have_ref[e * cols + d]
            turn = jnp.logical_and(here - there > cost, back < CAP).astype(jnp.int32)
            load_ref[d] = here - turn * cost
            load_ref[e] = there + turn * cost
            have_ref[e * cols + d] = back + turn
            turn_ref[p] = turn
        return 0

    lax.fori_loop(0, pairs_dev, weigh, 0)

    def lay(d, number):
        for j in range(pairs_dev):
            p = d * pairs_dev + j
            turn = turn_ref[p] == 1
            e = peer_ref[p]
            x = jnp.where(turn, e, d)
            y = jnp.where(turn, d, e)
            near = near_ref[p]
            far = far_ref[p]
            block_x = jnp.where(turn, far, near)
            block_y = jnp.where(turn, near, far)
            seen = used_ref[x * cols + y]
            used_ref[x * cols + y] = seen + 1
            ours = x == mine
            at = jnp.where(ours, number, SPARE)
            meta_ref[0, at] = block_x
            meta_ref[1, at] = y * CAP + seen
            meta_ref[2, at] = reach_ref[p]
            meta_ref[3, at] = y * count + block_y
            meta_ref[4, jnp.where(y == mine, x * CAP + seen, SPARE)] = block_y
            number = number + ours.astype(jnp.int32)
        return number

    meta_ref[5, 0] = lax.fori_loop(0, cols, lay, jnp.int32(0))


def spread_columns(rows):
    turned = jnp.transpose(rows)
    return [jnp.broadcast_to(turned[:, k:k + 1], (BLOCK, LANES)) for k in range(8)]


def rounded(values):
    return values.astype(BF16).astype(F32)


def per_system(ref):
    which = lax.broadcasted_iota(jnp.int32, (LS, LANES), 0)
    out = jnp.zeros((LS, LANES), F32)
    for l in range(LS):
        out = jnp.where(which == l, ref[l], out)
    return out


def wide(column, width):
    return jnp.concatenate([column] * (width // LANES), axis=1)


def lane_fold(values):
    total = values[:, 0:LANES]
    for c in range(1, values.shape[1] // LANES):
        total = total + values[:, c * LANES:(c + 1) * LANES]
    return total


def distance(col_refs, row_vals, width):
    summed = None
    for k in range(3):
        differ = wide(col_refs[k], width) - row_vals[k]
        square = differ * differ
        summed = square if summed is None else summed + square
    summed = jnp.maximum(summed, 1e-30)
    return summed * lax.rsqrt(summed)


CREST = 4.0**0.2


def kernel_value(dist, slope):
    remain = jnp.maximum(CREST - dist * slope, 0.0)
    squared = remain * remain
    return ((squared * squared) * (5.0 / CREST**4 - remain)).astype(BF16)


def sub_fold(values):
    return values[0:8, :] + values[8:16, :]


def fold_forward(forward_ref, s):
    lane = lax.broadcasted_iota(jnp.int32, (LANES, LANES), 1)
    out = []
    for part in range(BLOCK // LANES):
        held = jnp.zeros((LANES, LANES), F32)
        for l in range(LS):
            block = forward_ref[s, l, part * LANES:(part + 1) * LANES, :]
            held = jnp.where(lane == l, jnp.sum(block, axis=1, keepdims=True), held)
        out.append(jnp.transpose(held)[0:LS, :])
    return jnp.concatenate(out, axis=1)


def partner_rows(far_ref, which):
    both = far_ref[over(which, 2)]
    return jnp.where(rest(which, 2) == 1, both[4:8, :], both[0:4, :])


def own_kernel(common, ls_ref, loc_ref, vec_ref, out_ref, coord_ref, col_ref, dist_ref, forward_ref):
    count = loc_ref.shape[0]
    parts = BLOCK // LANES
    per = LANES // CHUNK

    def block(s, _):
        columns = spread_columns(loc_ref[s])
        for k in range(4):
            coord_ref[k] = columns[k]
        if common:
            coord_ref[3] = rounded(columns[3])
        else:
            columns = spread_columns(vec_ref[s])
            for l in range(LS):
                col_ref[l] = columns[l]
        for part in range(parts):
            low = part * LANES
            width = BLOCK - low
            rows = [loc_ref[s, k:k + 1, low:] for k in range(3)]

            def measure(c, _):
                at = pl.ds(pl.multiple_of(low + c * CHUNK, CHUNK), CHUNK)
                dist_ref[at, low:] = distance([coord_ref[k, at, :] for k in range(3)], rows, width)
                return 0

            lax.fori_loop(0, per, measure, 0, unroll=8)

        def two(t, _):
            back = [jnp.zeros((8, BLOCK), F32) for _ in range(2)]
            ids = [2 * t, 2 * t + 1]
            slopes = [ls_ref[l] for l in ids]
            for part in range(parts):
                low = part * LANES
                width = BLOCK - low
                if common:
                    rows = [rounded(loc_ref[s, 3:4, low:])] * 2
                else:
                    rows = [vec_ref[s, pl.ds(l, 1), :][:, low:] for l in ids]

                def step(c, held):
                    at = pl.ds(pl.multiple_of(low + c * CHUNK, CHUNK), CHUNK)
                    dist = dist_ref[at, low:]
                    fresh = []
                    for n in range(2):
                        value = kernel_value(dist, slopes[n]).astype(F32)
                        forward_ref[s, ids[n], at, :] = lane_fold(value * rows[n])
                        if width > LANES:
                            column = coord_ref[3, at, :] if common else col_ref[ids[n], at, :]
                            right = value[:, LANES:] * wide(column, width - LANES)
                            fresh.append(held[n] + sub_fold(right))
                    return tuple(fresh) if fresh else held

                start = max(width - LANES, LANES)
                held = tuple(jnp.zeros((8, start), F32) for _ in range(2))
                held = lax.fori_loop(0, per, step, held, unroll=8)
                if width > LANES:
                    for n in range(2):
                        back[n] = jnp.concatenate(
                            [back[n][:, :low + LANES], back[n][:, low + LANES:] + held[n]], axis=1
                        )
            for n in range(2):
                out_ref[s, pl.ds(ids[n], 1), :] = jnp.sum(back[n], axis=0, keepdims=True)
            return 0

        lax.fori_loop(0, LS // 2, two, 0)
        out_ref[s] = out_ref[s] + fold_forward(forward_ref, s)
        return 0

    lax.fori_loop(0, count, block, 0)


def first_kernel(
    ls_ref, meta_ref, loc_ref, far_ref,
    out_ref, back_ref, tiles_ref,
    coord_ref, dist_ref, forward_ref, stage_ref, sem_ref,
):
    count = loc_ref.shape[0]
    pair_count = meta_ref[5, 0]
    steps = BLOCK // CHUNK
    for s in range(count):
        columns = spread_columns(loc_ref[s])
        for k in range(3):
            coord_ref[s, k] = columns[k]
        coord_ref[s, 3] = rounded(columns[3])
    forward_ref[...] = jnp.zeros(forward_ref.shape, F32)

    def store_copy(slot, number):
        return pltpu.make_async_copy(stage_ref.at[slot], tiles_ref.at[number], sem_ref.at[slot])

    def pair(p, number):
        a = meta_ref[0, p]
        q = meta_ref[1, p]
        reach = meta_ref[2, p]
        mine = partner_rows(far_ref, meta_ref[3, p])
        rows = [mine[k:k + 1, :] for k in range(3)]
        values = rounded(mine[3:4, :])

        def measure(c, _):
            at = pl.ds(pl.multiple_of(c * CHUNK, CHUNK), CHUNK)
            dist_ref[at, :] = distance([coord_ref[a, k, at, :] for k in range(3)], rows, BLOCK)
            return 0

        lax.fori_loop(0, steps, measure, 0, unroll=8)
        back_ref[q] = jnp.zeros((LS, BLOCK), F32)

        def sweep(ids, number):
            slopes = [ls_ref[l] for l in ids]
            slots = [(number + n) % 4 for n in range(len(ids))]
            for n in range(len(ids)):
                @pl.when(number + n >= 4)
                def _():
                    store_copy(slots[n], number + n).wait()

            def step(c, held):
                at = pl.ds(pl.multiple_of(c * CHUNK, CHUNK), CHUNK)
                dist = dist_ref[at, :]
                column = wide(coord_ref[a, 3, at, :], BLOCK)
                fresh = []
                for n in range(len(ids)):
                    value = kernel_value(dist, slopes[n])
                    stage_ref[slots[n], at, :] = value
                    value = value.astype(F32)
                    forward_ref[a, ids[n], at, :] += lane_fold(value * values)
                    fresh.append(held[n] + sub_fold(value * column))
                return tuple(fresh)

            held = tuple(jnp.zeros((8, BLOCK), F32) for _ in ids)
            held = lax.fori_loop(0, steps, step, held, unroll=8)
            for n in range(len(ids)):
                back_ref[q, pl.ds(ids[n], 1), :] = jnp.sum(held[n], axis=0, keepdims=True)
                store_copy(slots[n], number + n).start()
            return number + len(ids)

        live = LS - reach

        def two(t, number):
            return sweep([LS - 1 - 2 * t, LS - 2 - 2 * t], number)

        number = lax.fori_loop(0, live // 2, two, number)
        return lax.cond(live % 2 == 1, lambda m: sweep([reach], m), lambda m: m, number)

    number = lax.fori_loop(0, pair_count, pair, jnp.int32(0))
    for back in range(4):
        @pl.when(number > back)
        def _():
            store_copy((number - 1 - back) % 4, number - 1 - back).wait()

    for s in range(count):
        out_ref[s] = fold_forward(forward_ref, s)


def combine_kernel(
    meta_ref, loc_ref, own_ref, fwd_ref, got_ref, w_ref, send_ref, dots_ref
):
    count = loc_ref.shape[0]
    slots = got_ref.shape[0]
    w_ref[...] = own_ref[...] + fwd_ref[...]
    for q in range(slots):
        where = meta_ref[4, q]

        @pl.when(where >= 0)
        def _():
            w_ref[where] = w_ref[where] + got_ref[q]

    unit = 1.0 / (2.0 * BLOCK)
    products = [jnp.zeros((LS, BLOCK), F32) for _ in range(3)]
    for s in range(count):
        value = w_ref[s] * unit
        w_ref[s] = value
        target = jnp.broadcast_to(loc_ref[s, 3:4, :], (LS, BLOCK))
        products[0] = products[0] + target * target
        products[1] = products[1] + target * value
        products[2] = products[2] + value * value
    for q in range(slots):
        send_ref[q] = w_ref[jnp.maximum(meta_ref[4, q], 0)]
    lane = lax.broadcasted_iota(jnp.int32, (LS, LANES), 1)
    held = jnp.zeros((LS, LANES), F32)
    for n in range(3):
        held = jnp.where(lane == n, jnp.sum(products[n], axis=1, keepdims=True), held)
    dots_ref[...] = held


def second_kernel(
    meta_ref, loc_ref, w_ref, own_ref, far_pts_ref, far_ref, dots_ref, tiles_ref,
    out_ref, back_ref,
    list_ref, col_ref, forward_ref, wz_ref, yz_ref, stage_ref, sem_ref,
):
    count = w_ref.shape[0]
    pair_count = meta_ref[5, 0]
    steps = BLOCK // CHUNK
    depth = stage_ref.shape[0]

    def list_pair(p, number):
        reach = meta_ref[2, p]
        live = LS - reach

        def two(t, number):
            list_ref[number] = p * LS + LS - 1 - t
            return number + 1

        return lax.fori_loop(0, live, two, number)

    number = lax.fori_loop(0, pair_count, list_pair, jnp.int32(0))

    def load_copy(t):
        slot = t % depth
        return pltpu.make_async_copy(tiles_ref.at[t], stage_ref.at[slot], sem_ref.at[slot])

    for t in range(depth - 1):
        @pl.when(t < number)
        def _():
            load_copy(jnp.int32(t)).start()


    def clear(p, _):
        q = meta_ref[1, p]
        back_ref[over(q, CAP), pl.ds(pl.multiple_of(rest(q, CAP) * LS, LS), LS), :BLOCK] = jnp.zeros((LS, BLOCK), F32)
        return 0

    lax.fori_loop(0, pair_count, clear, 0)
    for s in range(count):
        columns = spread_columns(w_ref[s])
        for l in range(LS):
            col_ref[s, l] = columns[l]
    forward_ref[...] = jnp.zeros(forward_ref.shape, F32)
    wz_ref[...] = jnp.zeros(wz_ref.shape, F32)
    yz_ref[...] = jnp.zeros(yz_ref.shape, F32)

    def tile(t, _):
        entry = list_ref[t]
        p = over(entry, LS)
        l = rest(entry, LS)
        a = meta_ref[0, p]
        q = meta_ref[1, p]
        slot = t % depth

        @pl.when(t + depth - 1 < number)
        def _():
            load_copy(t + depth - 1).start()

        load_copy(t).wait()
        row = far_ref[q, pl.ds(l, 1), :]

        def step(c, held):
            at = pl.ds(pl.multiple_of(c * CHUNK, CHUNK), CHUNK)
            value = stage_ref[slot, at, :].astype(F32)
            forward_ref[a, l, at, :] += lane_fold(value * row)
            return held + sub_fold(value * wide(col_ref[a, l, at, :], BLOCK))

        held = lax.fori_loop(0, steps, step, jnp.zeros((8, BLOCK), F32), unroll=32)
        result = jnp.sum(held, axis=0, keepdims=True)
        back_ref[over(q, CAP), pl.ds(rest(q, CAP) * LS + l, 1), :BLOCK] = result
        target = partner_rows(far_pts_ref, meta_ref[3, p])[3:4, :]
        wz_ref[pl.ds(l, 1), :] += result * row
        yz_ref[pl.ds(l, 1), :] += result * target
        return 0

    lax.fori_loop(0, number, tile, 0)
    wz = wz_ref[...]
    yz = yz_ref[...]
    for s in range(count):
        value = own_ref[s] + fold_forward(forward_ref, s)
        out_ref[s] = value
        wz = wz + value * w_ref[s]
        yz = yz + value * loc_ref[s, 3:4, :]
    unit = 1.0 / (2.0 * BLOCK)
    lane = lax.broadcasted_iota(jnp.int32, (LS, LANES), 1)
    held = jnp.where(lane == 3, jnp.sum(wz, axis=1, keepdims=True) * unit, dots_ref[...])
    held = jnp.where(lane == 4, jnp.sum(yz, axis=1, keepdims=True) * unit, held)
    for c in range(back_ref.shape[0]):
        back_ref[c, 0:LS, BLOCK:] = held


SPAN = LANES // LS


def system_lanes(n):
    sub = lax.broadcasted_iota(jnp.int32, (LS, LANES), 0)
    lane = lax.broadcasted_iota(jnp.int32, (LS, LANES), 1)
    return lane == sub * SPAN + n


def dots_kernel(got_ref, dots_ref):
    held = got_ref[0, 0:LS, :]
    for c in range(1, got_ref.shape[0]):
        held = held + got_ref[c, 0:LS, :]
    row = jnp.zeros((LS, LANES), F32)
    for n in range(DOTS):
        row = jnp.where(system_lanes(n), held[:, n:n + 1], row)
    row = jnp.sum(row, axis=0, keepdims=True)
    dots_ref[...] = jnp.broadcast_to(row, dots_ref.shape)


def gather_kernel(meta_ref, part_ref, got_ref, z_ref):
    z_ref[...] = part_ref[...]
    for c in range(got_ref.shape[0]):
        for k in range(CAP):
            where = meta_ref[4, c * CAP + k]

            @pl.when(where >= 0)
            def _():
                z_ref[where] = z_ref[where] + got_ref[c, k * LS:(k + 1) * LS, :BLOCK]

    z_ref[...] = z_ref[...] * (1.0 / (2.0 * BLOCK))


def finish_kernel(noise_ref, loc_ref, w_ref, z_ref, dots_ref, sol_ref, res_ref):
    row = jnp.sum(dots_ref[...], axis=0, keepdims=True)
    spread = jnp.broadcast_to(row, (LS, LANES))
    noise = per_system(noise_ref)[:, 0:1]
    yy, yw, ww, wz, yz = [
        jnp.sum(jnp.where(system_lanes(n), spread, 0.0), axis=1, keepdims=True) for n in range(DOTS)
    ]
    curve = noise * yy + yw
    first = yy / curve
    keep = yw / curve
    fresh = first * ((yy * ww - yw * yw) / curve)
    beta = fresh / yy
    gain = keep + beta
    bend = noise * fresh * (1.0 + beta) + gain * gain * yw - gain * first * (ww + yz) + first * first * wz
    second = fresh / bend
    sol_y = first + second * gain
    sol_w = second * first
    res_y = keep - second * noise * gain
    res_w = second * (noise * first - gain) - first
    for s in range(loc_ref.shape[0]):
        target = loc_ref[s, 3:4, :]
        value = w_ref[s]
        sol_ref[:, s * BLOCK:(s + 1) * BLOCK] = sol_y * target - sol_w * value
        res_ref[:, s * BLOCK:(s + 1) * BLOCK] = res_y * target + res_w * value + sol_w * z_ref[s]


def on_device(points, targets, kd_order, lengthscales, noise_level, block_owner, block_pairs):
    cols = lax.axis_size("col")
    rows = lax.axis_size("row")
    me = (lax.axis_index("row") * cols + lax.axis_index("col")).astype(jnp.int32).reshape(1)
    total = points.shape[1]
    count = total // BLOCK
    pairs_dev = block_pairs.shape[1] // (rows * cols)
    slots = cols * CAP
    most = (cols - 1) * CAP * LS
    field = jax.ShapeDtypeStruct((count, LS, BLOCK), F32)

    loc, send = pl.pallas_call(
        order_kernel,
        out_shape=(
            jax.ShapeDtypeStruct((count, 8, BLOCK), F32),
            jax.ShapeDtypeStruct((cols * (count // 2), 8, BLOCK), F32),
        ),
        in_specs=[vmem_spec()] * 3,
        out_specs=(vmem_spec(),) * 2,
        compiler_params=params(),
        name="order",
    )(points, targets.reshape(1, total), kd_order.reshape(1, total))
    meta = pl.pallas_call(
        lambda *refs: plan_kernel(cols, count, pairs_dev, *refs),
        out_shape=jax.ShapeDtypeStruct((8, SPARE + 1), jnp.int32),
        in_specs=[smem_spec()] * 3,
        out_specs=smem_spec(),
        scratch_shapes=[
            *[SMEM((cols * pairs_dev,), jnp.int32)] * 5,
            SMEM((cols,), jnp.int32),
            SMEM((cols * cols,), jnp.int32),
            SMEM((cols * cols,), jnp.int32),
        ],
        compiler_params=params(),
        cost_estimate=pl.CostEstimate(flops=10**9, bytes_accessed=10**6, transcendentals=0),
        name="plan",
    )(me, block_owner, block_pairs)

    slopes = CREST / lengthscales

    def own(vec, common):
        return pl.pallas_call(
            lambda *refs: own_kernel(common, *refs),
            out_shape=field,
            in_specs=[smem_spec(), vmem_spec(), vmem_spec()],
            out_specs=vmem_spec(),
            scratch_shapes=[
                VMEM((4, BLOCK, LANES), F32),
                VMEM((LS, BLOCK, LANES), F32),
                VMEM((BLOCK, BLOCK), F32),
                VMEM((count, LS, BLOCK, LANES), F32),
            ],
            compiler_params=params(),
            cost_estimate=pl.CostEstimate(flops=2 * 10**9, bytes_accessed=10**6, transcendentals=0),
            name="own_first" if common else "own_second",
        )(slopes, loc, vec)

    far = lax.all_to_all(send, "col", split_axis=0, concat_axis=0, tiled=True)
    own_one = own(loc, True)
    fwd_one, back_one, tiles = pl.pallas_call(
        first_kernel,
        out_shape=(
            field,
            jax.ShapeDtypeStruct((slots, LS, BLOCK), F32),
            jax.ShapeDtypeStruct((most, BLOCK, BLOCK), BF16),
        ),
        in_specs=[smem_spec(), smem_spec(), vmem_spec(), vmem_spec()],
        out_specs=(vmem_spec(), vmem_spec(), any_spec()),
        scratch_shapes=[
            VMEM((count, 4, BLOCK, LANES), F32),
            VMEM((BLOCK, BLOCK), F32),
            VMEM((count, LS, BLOCK, LANES), F32),
            VMEM((4, BLOCK, BLOCK), BF16),
            pltpu.SemaphoreType.DMA((4,)),
        ],
        compiler_params=params(),
        cost_estimate=pl.CostEstimate(flops=10**10, bytes_accessed=6 * 10**7, transcendentals=0),
        name="cross_first",
    )(slopes, meta, loc, far)
    got_one = lax.all_to_all(back_one, "col", split_axis=0, concat_axis=0, tiled=True)

    w, send_w, dots_one = pl.pallas_call(
        combine_kernel,
        out_shape=(
            field,
            jax.ShapeDtypeStruct((slots, LS, BLOCK), F32),
            jax.ShapeDtypeStruct((LS, LANES), F32),
        ),
        in_specs=[smem_spec()] + [vmem_spec()] * 4,
        out_specs=(vmem_spec(),) * 3,
        compiler_params=params(),
        name="combine",
    )(meta, loc, own_one, fwd_one, got_one)
    far_w = lax.all_to_all(send_w, "col", split_axis=0, concat_axis=0, tiled=True)
    own_two = own(w, False)
    fwd_two, back_two = pl.pallas_call(
        second_kernel,
        out_shape=(field, jax.ShapeDtypeStruct((cols, CAP * LS, BLOCK + LANES), F32)),
        in_specs=[smem_spec()] + [vmem_spec()] * 6 + [any_spec()],
        out_specs=(vmem_spec(),) * 2,
        scratch_shapes=[
            SMEM((most,), jnp.int32),
            VMEM((count, LS, BLOCK, LANES), F32),
            VMEM((count, LS, BLOCK, LANES), F32),
            VMEM((LS, BLOCK), F32),
            VMEM((LS, BLOCK), F32),
            VMEM((8, BLOCK, BLOCK), BF16),
            pltpu.SemaphoreType.DMA((8,)),
        ],
        compiler_params=params(),
        cost_estimate=pl.CostEstimate(flops=5 * 10**9, bytes_accessed=6 * 10**7, transcendentals=0),
        name="cross_second",
    )(meta, loc, w, own_two, far, far_w, dots_one, tiles)
    got_two = lax.all_to_all(back_two, "col", split_axis=0, concat_axis=0, tiled=True)

    dots_two = pl.pallas_call(
        dots_kernel,
        out_shape=jax.ShapeDtypeStruct((rows, LANES), F32),
        in_specs=[pl.BlockSpec((cols, LS, LANES), lambda i: (0, 0, BLOCK // LANES))],
        out_specs=pl.BlockSpec((rows, LANES), lambda i: (0, 0)),
        grid=(1,),
        compiler_params=params(),
        name="dots",
    )(got_two)
    dots = lax.all_to_all(dots_two, "row", split_axis=0, concat_axis=0, tiled=True)
    z = pl.pallas_call(
        gather_kernel,
        out_shape=field,
        in_specs=[smem_spec()] + [vmem_spec()] * 2,
        out_specs=vmem_spec(),
        compiler_params=params(),
        cost_estimate=pl.CostEstimate(flops=10**8, bytes_accessed=2 * 10**6, transcendentals=0),
        name="gather",
    )(meta, fwd_two, got_two)
    return pl.pallas_call(
        finish_kernel,
        out_shape=(jax.ShapeDtypeStruct((LS, total), F32),) * 2,
        in_specs=[smem_spec()] + [vmem_spec()] * 4,
        out_specs=(vmem_spec(),) * 2,
        compiler_params=params(),
        name="finish",
    )(noise_level, loc, w, z, dots)


def solution(mesh):
    placed = (P(None, ("row", "col")), P(("row", "col")), P(("row", "col")), P(), P(), P(), P())
    return jax.shard_map(
        on_device,
        mesh=mesh,
        in_specs=placed,
        out_specs=(P(None, ("row", "col")), P(None, ("row", "col"))),
        check_vma=False,
    )
```

```python
import jax
import jax.numpy as jnp
from jax import lax
from jax.experimental import pallas as pl
from jax.experimental.pallas import tpu as pltpu
from jax.sharding import PartitionSpec as P

BLOCK = 512
LS = 8
CAP = 2
LANES = 128
CHUNK = 16
DOTS = 5
F32 = jnp.float32
BF16 = jnp.bfloat16
VMEM = pltpu.VMEM
SMEM = pltpu.SMEM


def vmem_spec():
    return pl.BlockSpec(memory_space=pltpu.VMEM)


def smem_spec():
    return pl.BlockSpec(memory_space=pltpu.SMEM)


def any_spec():
    return pl.BlockSpec(memory_space=pl.ANY)


def hbm_spec():
    return pl.BlockSpec(memory_space=pltpu.HBM)


def start_copies(sources, targets, sems):
    copies = [pltpu.make_async_copy(a, b, sems.at[n]) for n, (a, b) in enumerate(zip(sources, targets))]
    for copy in copies:
        copy.start()
    return copies


def params(mebibytes):
    return pltpu.CompilerParams(vmem_limit_bytes=mebibytes * 2**20)


def over(value, size):
    return value >> (size.bit_length() - 1) if size & (size - 1) == 0 else value // size


def rest(value, size):
    return value & (size - 1) if size & (size - 1) == 0 else value % size


def order_kernel(pts_hbm, tgt_hbm, order_hbm, loc_ref, send_ref, pts_ref, tgt_ref, order_ref, sems):
    for copy in start_copies((pts_hbm, tgt_hbm, order_hbm), (pts_ref, tgt_ref, order_ref), sems):
        copy.wait()
    total = pts_ref.shape[1]
    pieces = total // LANES
    per = BLOCK // LANES
    source = jnp.concatenate([pts_ref[...], tgt_ref[...], jnp.zeros((4, total), F32)], axis=0)
    for o in range(pieces):
        index = jnp.broadcast_to(order_ref[:, o * LANES:(o + 1) * LANES], (8, LANES))
        high = over(index, LANES)
        low = rest(index, LANES)
        got = jnp.zeros((8, LANES), F32)
        for c in range(pieces):
            part = jnp.take_along_axis(
                source[:, c * LANES:(c + 1) * LANES], low, axis=1, mode="promise_in_bounds"
            )
            got = jnp.where(high == c, part, got)
        loc_ref[o // per, :, (o % per) * LANES:(o % per + 1) * LANES] = got
    halves = []
    for h in range(loc_ref.shape[0] // 2):
        halves.append(jnp.concatenate([loc_ref[2 * h, 0:4, :], loc_ref[2 * h + 1, 0:4, :]], axis=0))
    for c in range(send_ref.shape[0] // len(halves)):
        for h in range(len(halves)):
            send_ref[c * len(halves) + h] = halves[h]


SPARE = 63


def plan_kernel(cols, count, pairs_dev, me_ref, owner_hbm, pairs_hbm, meta_ref, peer_ref, cost_ref, turn_ref, load_ref, have_ref, asking_ref, used_ref, owner_ref, pairs_ref, sems):
    copies = start_copies((owner_hbm, pairs_hbm), (owner_ref, pairs_ref), sems)
    mine = rest(me_ref[0], cols)
    start = over(me_ref[0], cols) * (cols * pairs_dev)

    def clear(i, _):
        for c in range(cols):
            have_ref[i * cols + c] = 0
        for c in range(4):
            used_ref[c * cols + i] = 0
        return 0

    lax.fori_loop(0, cols, clear, 0)
    for q in range(cols * CAP):
        meta_ref[4, q] = -1
    for copy in copies:
        copy.wait()

    def read(d, asking):
        total = jnp.int32(0)
        for j in range(pairs_dev):
            p = d * pairs_dev + j
            e = rest(over(owner_ref[pairs_ref[1, start + p]], count), cols)
            cost = 4 * (LS - pairs_ref[2, start + p]) + 3
            peer_ref[p] = e
            cost_ref[p] = cost
            total = total + cost
            have_ref[d * cols + e] = have_ref[d * cols + e] + 1
            asking_ref[asking] = p
            asking = asking + (e == mine).astype(jnp.int32)
        load_ref[d] = total
        return asking

    asking = lax.fori_loop(0, cols, read, jnp.int32(0))

    def weigh(j, _):
        for d in range(cols):
            p = d * pairs_dev + j
            e = peer_ref[p]
            cost = cost_ref[p]
            here = load_ref[d]
            there = load_ref[e]
            back = have_ref[e * cols + d]
            turn = jnp.logical_and(here - there > cost, back < CAP).astype(jnp.int32)
            load_ref[d] = here - turn * cost
            load_ref[e] = there + turn * cost
            have_ref[e * cols + d] = back + turn
            turn_ref[p] = turn
        return 0

    lax.fori_loop(0, pairs_dev, weigh, 0)

    def lay(p, other, here, number):
        turn = turn_ref[p]
        turned = turn == 1
        near = rest(owner_ref[pairs_ref[0, start + p]], count)
        far = rest(owner_ref[pairs_ref[1, start + p]], count)
        at_used = (2 * here + turn) * cols + other
        seen = used_ref[at_used]
        used_ref[at_used] = seen + 1
        slot = other * CAP + jnp.where(turned, CAP - 1 - seen, seen)
        ours = turn == here
        mine_block, their_block = (far, near) if here else (near, far)
        at = jnp.where(ours, number, SPARE)
        meta_ref[0, at] = mine_block
        meta_ref[1, at] = slot
        meta_ref[2, at] = pairs_ref[2, start + p]
        meta_ref[3, at] = other * count + their_block
        meta_ref[4, jnp.where(ours, SPARE, slot)] = mine_block
        return number + ours.astype(jnp.int32)

    number = jnp.int32(0)
    for j in range(pairs_dev):
        p = mine * pairs_dev + j
        number = lay(p, peer_ref[p], 0, number)

    def lay_asking(i, number):
        p = asking_ref[i]
        return lay(p, over(p, pairs_dev), 1, number)

    meta_ref[5, 0] = lax.fori_loop(0, asking, lay_asking, number)


def spread_columns(rows):
    turned = jnp.transpose(rows)
    return [jnp.broadcast_to(turned[:, k:k + 1], (BLOCK, LANES)) for k in range(8)]


def rounded(values):
    return values.astype(BF16).astype(F32)


def per_system(ref):
    which = lax.broadcasted_iota(jnp.int32, (LS, LANES), 0)
    out = jnp.zeros((LS, LANES), F32)
    for l in range(LS):
        out = jnp.where(which == l, ref[l], out)
    return out


def wide(column, width):
    return jnp.concatenate([column] * (width // LANES), axis=1)


def lane_fold(values):
    total = values[:, 0:LANES]
    for c in range(1, values.shape[1] // LANES):
        total = total + values[:, c * LANES:(c + 1) * LANES]
    return total


def distance(col_refs, row_vals, width):
    summed = None
    for k in range(3):
        differ = wide(col_refs[k], width) - row_vals[k]
        square = differ * differ
        summed = square if summed is None else summed + square
    summed = jnp.maximum(summed, 1e-30)
    return summed * lax.rsqrt(summed)


CREST = 4.0**0.2


def slope_of(scale):
    one = CREST / jnp.full((8, LANES), scale, F32)
    return jnp.concatenate([one] * (CHUNK // 8), axis=0)


def kernel_value(dist, slope):
    remain = jnp.maximum(CREST - dist * wide(slope, dist.shape[1]), 0.0)
    squared = remain * remain
    return ((squared * squared) * (5.0 / CREST**4 - remain)).astype(BF16)


def sub_fold(values):
    return values[0:8, :] + values[8:16, :]


def fold_forward(forward_ref, s):
    lane = lax.broadcasted_iota(jnp.int32, (LANES, LANES), 1)
    out = []
    for part in range(BLOCK // LANES):
        held = jnp.zeros((LANES, LANES), F32)
        for l in range(LS):
            block = forward_ref[s, l, part * LANES:(part + 1) * LANES, :]
            held = jnp.where(lane == l, jnp.sum(block, axis=1, keepdims=True), held)
        out.append(jnp.transpose(held)[0:LS, :])
    return jnp.concatenate(out, axis=1)


def partner_rows(far_ref, which):
    both = far_ref[over(which, 2)]
    return jnp.where(rest(which, 2) == 1, both[4:8, :], both[0:4, :])


def own_tiles(common, s, ls_ref, loc_ref, vec_ref, coord_ref, col_ref, dist_ref, forward_ref, out_ref):
    parts = BLOCK // LANES
    per = LANES // CHUNK
    turns = LS // 2
    for part in range(parts):
        low = part * LANES
        width = BLOCK - low
        rows = [loc_ref[s, k:k + 1, low:] for k in range(3)]

        def measure(c, _):
            at = pl.ds(pl.multiple_of(low + c * CHUNK, CHUNK), CHUNK)
            dist_ref[at, low:] = distance([coord_ref[k, at, :] for k in range(3)], rows, width)
            return 0

        lax.fori_loop(0, per, measure, 0, unroll=8)

    def two(t, _):
        back = [jnp.zeros((8, BLOCK), F32) for _ in range(2)]
        ids = [2 * t, 2 * t + 1]
        slopes = [slope_of(ls_ref[l]) for l in ids]
        for part in range(parts):
            low = part * LANES
            width = BLOCK - low
            if common:
                rows = [rounded(loc_ref[s, 3:4, low:])] * 2
            else:
                rows = [vec_ref[s, pl.ds(l, 1), :][:, low:] for l in ids]

            def step(c, held):
                at = slice(low + c * CHUNK, low + (c + 1) * CHUNK)
                dist = dist_ref[at, low:]
                fresh = []
                for n in range(2):
                    value = kernel_value(dist, slopes[n]).astype(F32)
                    forward_ref[ids[n], at, :] = lane_fold(value * rows[n])
                    if width > LANES:
                        column = coord_ref[3, at, :] if common else col_ref[ids[n], at, :]
                        right = value[:, LANES:] * wide(column, width - LANES)
                        fresh.append(held[n] + sub_fold(right))
                return tuple(fresh) if fresh else held

            start = max(width - LANES, LANES)
            held = tuple(jnp.zeros((8, start), F32) for _ in range(2))
            for c in range(per):
                held = step(c, held)
            if width > LANES:
                for n in range(2):
                    back[n] = jnp.concatenate(
                        [back[n][:, :low + LANES], back[n][:, low + LANES:] + held[n]], axis=1
                    )
        for n in range(2):
            out_ref[pl.ds(ids[n], 1), :] = jnp.sum(back[n], axis=0, keepdims=True)
        return 0

    lax.fori_loop(0, turns, two, 0)


def own_kernel(common, ls_hbm, loc_ref, vec_ref, out_ref, coord_ref, col_ref, dist_ref, forward_ref, ls_ref, sems):
    (ls_copy,) = start_copies((ls_hbm,), (ls_ref,), sems)
    columns = spread_columns(loc_ref[0])
    for k in range(4):
        coord_ref[k] = columns[k]
    if common:
        coord_ref[3] = rounded(columns[3])
    else:
        columns = spread_columns(vec_ref[0])
        for l in range(LS):
            col_ref[l] = columns[l]
    ls_copy.wait()
    own_tiles(common, 0, ls_ref, loc_ref, vec_ref, coord_ref, col_ref, dist_ref, forward_ref.at[0], out_ref.at[0])
    out_ref[0] = out_ref[0] + fold_forward(forward_ref, 0)


def first_kernel(
    ls_hbm, meta_ref, loc_ref, far_hbm_ref,
    out_ref, back_ref, tiles_ref,
    coord_ref, dist_ref, forward_ref, stage_ref, far_ref, ls_ref, sem_ref, far_sem,
):
    count = loc_ref.shape[0]
    pair_count = meta_ref[5, 0]
    steps = BLOCK // CHUNK
    far_copy, ls_copy = start_copies((far_hbm_ref, ls_hbm), (far_ref, ls_ref), far_sem)
    for s in range(count):
        columns = spread_columns(loc_ref[s])
        for k in range(3):
            coord_ref[s, k] = columns[k]
        coord_ref[s, 3] = rounded(columns[3])
    forward_ref[0] = jnp.zeros(forward_ref.shape[1:], F32)
    out_ref[0] = jnp.zeros(out_ref.shape[1:], F32)

    def own(s, _):
        own_tiles(
            True, s, ls_ref, loc_ref, None, coord_ref.at[s], None, dist_ref, forward_ref.at[s], out_ref.at[s]
        )
        return 0

    ls_copy.wait()
    lax.fori_loop(1, count, own, 0)
    far_copy.wait()

    def store_copy(slot, number):
        return pltpu.make_async_copy(stage_ref.at[slot], tiles_ref.at[number], sem_ref.at[slot])

    def pair(p, number):
        a = meta_ref[0, p]
        q = meta_ref[1, p]
        reach = meta_ref[2, p]
        mine = partner_rows(far_ref, meta_ref[3, p])
        rows = [mine[k:k + 1, :] for k in range(3)]
        values = rounded(mine[3:4, :])

        def measure(c, _):
            at = pl.ds(pl.multiple_of(c * CHUNK, CHUNK), CHUNK)
            dist_ref[at, :] = distance([coord_ref[a, k, at, :] for k in range(3)], rows, BLOCK)
            return 0

        lax.fori_loop(0, steps, measure, 0, unroll=8)
        back_ref[q] = jnp.zeros((LS, BLOCK), F32)

        def sweep(ids, number):
            slopes = [slope_of(ls_ref[l]) for l in ids]
            slots = [(number + n) % 4 for n in range(len(ids))]
            for n in range(len(ids)):
                @pl.when(number + n >= 4)
                def _():
                    store_copy(slots[n], number + n).wait()

            def step(c, held):
                at = pl.ds(pl.multiple_of(c * CHUNK, CHUNK), CHUNK)
                dist = dist_ref[at, :]
                column = wide(coord_ref[a, 3, at, :], BLOCK)
                fresh = []
                for n in range(len(ids)):
                    value = kernel_value(dist, slopes[n])
                    stage_ref[slots[n], at, :] = value
                    value = value.astype(F32)
                    forward_ref[a, ids[n], at, :] += lane_fold(value * values)
                    fresh.append(held[n] + sub_fold(value * column))
                return tuple(fresh)

            held = tuple(jnp.zeros((8, BLOCK), F32) for _ in ids)
            held = lax.fori_loop(0, steps, step, held, unroll=8)
            for n in range(len(ids)):
                back_ref[q, pl.ds(ids[n], 1), :] = jnp.sum(held[n], axis=0, keepdims=True)
                store_copy(slots[n], number + n).start()
            return number + len(ids)

        live = LS - reach

        def two(t, number):
            return sweep([LS - 1 - 2 * t, LS - 2 - 2 * t], number)

        number = lax.fori_loop(0, live // 2, two, number)
        return lax.cond(live % 2 == 1, lambda m: sweep([reach], m), lambda m: m, number)

    number = lax.fori_loop(0, pair_count, pair, jnp.int32(0))
    for back in range(4):
        @pl.when(number > back)
        def _():
            store_copy((number - 1 - back) % 4, number - 1 - back).wait()

    for s in range(count):
        out_ref[s] = out_ref[s] + fold_forward(forward_ref, s)


def combine_kernel(
    meta_ref, loc_ref, own_ref, fwd_ref, got_ref, w_ref, send_ref, dots_ref
):
    count = loc_ref.shape[0]
    slots = got_ref.shape[0]
    w_ref[...] = fwd_ref[...]
    w_ref[0] = w_ref[0] + own_ref[0]
    for q in range(slots):
        where = meta_ref[4, q]

        @pl.when(where >= 0)
        def _():
            w_ref[where] = w_ref[where] + got_ref[q]

    unit = 1.0 / (2.0 * BLOCK)
    products = [jnp.zeros((LS, BLOCK), F32) for _ in range(3)]
    for s in range(count):
        value = w_ref[s] * unit
        w_ref[s] = value
        target = jnp.broadcast_to(loc_ref[s, 3:4, :], (LS, BLOCK))
        products[0] = products[0] + target * target
        products[1] = products[1] + target * value
        products[2] = products[2] + value * value
    for q in range(slots):
        send_ref[q] = w_ref[jnp.maximum(meta_ref[4, q], 0)]
    lane = lax.broadcasted_iota(jnp.int32, (LS, LANES), 1)
    held = jnp.zeros((LS, LANES), F32)
    for n in range(3):
        held = jnp.where(lane == n, jnp.sum(products[n], axis=1, keepdims=True), held)
    dots_ref[...] = held


def second_kernel(
    ls_hbm, meta_ref, loc_ref, w_ref, own_ref, dots_ref, far_pts_hbm_ref, far_hbm_ref, tiles_ref,
    out_ref, back_ref,
    list_ref, coord_ref, col_ref, dist_ref, forward_ref, wz_ref, yz_ref, stage_ref, far_pts_ref, far_ref,
    ls_ref, sem_ref, far_sem,
):
    count = w_ref.shape[0]
    pair_count = meta_ref[5, 0]
    steps = BLOCK // CHUNK
    depth = stage_ref.shape[0]
    *copies, ls_copy = start_copies(
        (far_pts_hbm_ref, far_hbm_ref, ls_hbm), (far_pts_ref, far_ref, ls_ref), far_sem
    )

    def list_pair(p, number):
        reach = meta_ref[2, p]
        live = LS - reach

        def two(t, number):
            list_ref[number] = p * LS + LS - 1 - t
            return number + 1

        return lax.fori_loop(0, live, two, number)

    number = lax.fori_loop(0, pair_count, list_pair, jnp.int32(0))

    def load_copy(t):
        slot = t % depth
        return pltpu.make_async_copy(tiles_ref.at[t], stage_ref.at[slot], sem_ref.at[slot])

    for t in range(depth - 1):
        @pl.when(t < number)
        def _():
            load_copy(jnp.int32(t)).start()


    def clear(p, _):
        q = meta_ref[1, p]
        back_ref[over(q, CAP), pl.ds(pl.multiple_of(rest(q, CAP) * LS, LS), LS), :BLOCK] = jnp.zeros((LS, BLOCK), F32)
        return 0

    lax.fori_loop(0, pair_count, clear, 0)
    for s in range(count):
        columns = spread_columns(w_ref[s])
        for l in range(LS):
            col_ref[s, l] = columns[l]
    forward_ref[0] = jnp.zeros(forward_ref.shape[1:], F32)
    out_ref[0] = own_ref[0]

    def own(s, _):
        columns = spread_columns(loc_ref[s])
        for k in range(3):
            coord_ref[k] = columns[k]
        own_tiles(
            False, s, ls_ref, loc_ref, w_ref, coord_ref, col_ref.at[s], dist_ref, forward_ref.at[s], out_ref.at[s]
        )
        return 0

    ls_copy.wait()
    lax.fori_loop(1, count, own, 0)
    for copy in copies:
        copy.wait()
    wz_ref[...] = jnp.zeros(wz_ref.shape, F32)
    yz_ref[...] = jnp.zeros(yz_ref.shape, F32)

    def tile(t, _):
        entry = list_ref[t]
        p = over(entry, LS)
        l = rest(entry, LS)
        a = meta_ref[0, p]
        q = meta_ref[1, p]
        slot = t % depth

        @pl.when(t + depth - 1 < number)
        def _():
            load_copy(t + depth - 1).start()

        load_copy(t).wait()
        row = far_ref[q, pl.ds(l, 1), :]

        def step(c, held):
            at = pl.ds(pl.multiple_of(c * CHUNK, CHUNK), CHUNK)
            value = stage_ref[slot, at, :].astype(F32)
            forward_ref[a, l, at, :] += lane_fold(value * row)
            return held + sub_fold(value * wide(col_ref[a, l, at, :], BLOCK))

        held = lax.fori_loop(0, steps, step, jnp.zeros((8, BLOCK), F32), unroll=32)
        result = jnp.sum(held, axis=0, keepdims=True)
        back_ref[over(q, CAP), pl.ds(rest(q, CAP) * LS + l, 1), :BLOCK] = result
        target = partner_rows(far_pts_ref, meta_ref[3, p])[3:4, :]
        wz_ref[pl.ds(l, 1), :] += result * row
        yz_ref[pl.ds(l, 1), :] += result * target
        return 0

    lax.fori_loop(0, number, tile, 0)
    wz = wz_ref[...]
    yz = yz_ref[...]
    for s in range(count):
        value = out_ref[s] + fold_forward(forward_ref, s)
        out_ref[s] = value
        wz = wz + value * w_ref[s]
        yz = yz + value * loc_ref[s, 3:4, :]
    unit = 1.0 / (2.0 * BLOCK)
    lane = lax.broadcasted_iota(jnp.int32, (LS, LANES), 1)
    held = jnp.where(lane == 3, jnp.sum(wz, axis=1, keepdims=True) * unit, dots_ref[...])
    held = jnp.where(lane == 4, jnp.sum(yz, axis=1, keepdims=True) * unit, held)
    for c in range(back_ref.shape[0]):
        back_ref[c, 0:LS, BLOCK:] = held


SPAN = LANES // LS


def system_lanes(n):
    sub = lax.broadcasted_iota(jnp.int32, (LS, LANES), 0)
    lane = lax.broadcasted_iota(jnp.int32, (LS, LANES), 1)
    return lane == sub * SPAN + n


def dots_kernel(got_ref, dots_ref):
    held = got_ref[0, 0:LS, :]
    for c in range(1, got_ref.shape[0]):
        held = held + got_ref[c, 0:LS, :]
    row = jnp.zeros((LS, LANES), F32)
    for n in range(DOTS):
        row = jnp.where(system_lanes(n), held[:, n:n + 1], row)
    row = jnp.sum(row, axis=0, keepdims=True)
    dots_ref[...] = jnp.broadcast_to(row, dots_ref.shape)


def gather_kernel(meta_ref, part_ref, got_ref, z_ref):
    z_ref[...] = part_ref[...]
    for c in range(got_ref.shape[0]):
        for k in range(CAP):
            where = meta_ref[4, c * CAP + k]

            @pl.when(where >= 0)
            def _():
                z_ref[where] = z_ref[where] + got_ref[c, k * LS:(k + 1) * LS, :BLOCK]

    z_ref[...] = z_ref[...] * (1.0 / (2.0 * BLOCK))


def finish_kernel(noise_ref, loc_ref, w_ref, z_ref, dots_ref, sol_ref, res_ref):
    row = jnp.sum(dots_ref[...], axis=0, keepdims=True)
    spread = jnp.broadcast_to(row, (LS, LANES))
    noise = per_system(noise_ref)[:, 0:1]
    yy, yw, ww, wz, yz = [
        jnp.sum(jnp.where(system_lanes(n), spread, 0.0), axis=1, keepdims=True) for n in range(DOTS)
    ]
    curve = noise * yy + yw
    first = yy / curve
    keep = yw / curve
    fresh = first * ((yy * ww - yw * yw) / curve)
    beta = fresh / yy
    gain = keep + beta
    bend = noise * fresh * (1.0 + beta) + gain * gain * yw - gain * first * (ww + yz) + first * first * wz
    second = fresh / bend
    sol_y = first + second * gain
    sol_w = second * first
    res_y = keep - second * noise * gain
    res_w = second * (noise * first - gain) - first
    for s in range(loc_ref.shape[0]):
        target = loc_ref[s, 3:4, :]
        value = w_ref[s]
        sol_ref[:, s * BLOCK:(s + 1) * BLOCK] = sol_y * target - sol_w * value
        res_ref[:, s * BLOCK:(s + 1) * BLOCK] = res_y * target + res_w * value + sol_w * z_ref[s]


def on_device(points, targets, kd_order, lengthscales, noise_level, block_owner, block_pairs):
    cols = lax.axis_size("col")
    rows = lax.axis_size("row")
    me = (lax.axis_index("row") * cols + lax.axis_index("col")).astype(jnp.int32).reshape(1)
    total = points.shape[1]
    count = total // BLOCK
    pairs_dev = block_pairs.shape[1] // (rows * cols)
    slots = cols * CAP
    most = (cols - 1) * CAP * LS
    field = jax.ShapeDtypeStruct((count, LS, BLOCK), F32)

    loc, send = pl.pallas_call(
        order_kernel,
        out_shape=(
            jax.ShapeDtypeStruct((count, 8, BLOCK), F32),
            jax.ShapeDtypeStruct((cols * (count // 2), 8, BLOCK), F32),
        ),
        in_specs=[hbm_spec()] * 3,
        out_specs=(vmem_spec(),) * 2,
        scratch_shapes=[
            VMEM((3, total), F32),
            VMEM((1, total), F32),
            VMEM((1, total), jnp.int32),
            pltpu.SemaphoreType.DMA((3,)),
        ],
        compiler_params=params(8),
        name="order",
    )(points, targets.reshape(1, total), kd_order.reshape(1, total))
    def own(vec, common):
        return pl.pallas_call(
            lambda *refs: own_kernel(common, *refs),
            out_shape=jax.ShapeDtypeStruct((1, LS, BLOCK), F32),
            in_specs=[hbm_spec(), vmem_spec(), vmem_spec()],
            out_specs=vmem_spec(),
            scratch_shapes=[
                VMEM((4, BLOCK, LANES), F32),
                VMEM((LS, BLOCK, LANES), F32),
                VMEM((BLOCK, BLOCK), F32),
                VMEM((1, LS, BLOCK, LANES), F32),
                SMEM((LS,), F32),
                pltpu.SemaphoreType.DMA((1,)),
            ],
            compiler_params=params(16),
            cost_estimate=pl.CostEstimate(flops=2 * 10**9, bytes_accessed=10**6, transcendentals=0),
            name="own_first" if common else "own_second",
        )(lengthscales, loc, vec)

    far = lax.all_to_all(send, "col", split_axis=0, concat_axis=0, tiled=True)
    meta = pl.pallas_call(
        lambda *refs: plan_kernel(cols, count, pairs_dev, *refs),
        out_shape=jax.ShapeDtypeStruct((8, SPARE + 1), jnp.int32),
        in_specs=[smem_spec(), hbm_spec(), hbm_spec()],
        out_specs=smem_spec(),
        scratch_shapes=[
            SMEM((n,), jnp.int32)
            for n in [cols * pairs_dev] * 3 + [cols, cols * cols, cols * pairs_dev + 1, 4 * cols]
        ] + [
            SMEM(block_owner.shape, jnp.int32),
            SMEM(block_pairs.shape, jnp.int32),
            pltpu.SemaphoreType.DMA((2,)),
        ],
        compiler_params=params(8),
        cost_estimate=pl.CostEstimate(flops=10**9, bytes_accessed=10**6, transcendentals=0),
        name="plan",
    )(me, block_owner, block_pairs)
    own_one = own(loc, True)
    fwd_one, back_one, tiles = pl.pallas_call(
        first_kernel,
        out_shape=(
            field,
            jax.ShapeDtypeStruct((slots, LS, BLOCK), F32),
            jax.ShapeDtypeStruct((most, BLOCK, BLOCK), BF16),
        ),
        in_specs=[hbm_spec(), smem_spec(), vmem_spec(), any_spec()],
        out_specs=(vmem_spec(), vmem_spec(), any_spec()),
        scratch_shapes=[
            VMEM((count, 4, BLOCK, LANES), F32),
            VMEM((BLOCK, BLOCK), F32),
            VMEM((count, LS, BLOCK, LANES), F32),
            VMEM((4, BLOCK, BLOCK), BF16),
            VMEM((slots, LS, BLOCK), F32),
            SMEM((LS,), F32),
            pltpu.SemaphoreType.DMA((4,)),
            pltpu.SemaphoreType.DMA((2,)),
        ],
        compiler_params=params(28),
        cost_estimate=pl.CostEstimate(flops=10**10, bytes_accessed=6 * 10**7, transcendentals=0),
        name="cross_first",
    )(lengthscales, meta, loc, far)
    got_one = lax.all_to_all(back_one, "col", split_axis=0, concat_axis=0, tiled=True)

    w, send_w, dots_one = pl.pallas_call(
        combine_kernel,
        out_shape=(
            field,
            jax.ShapeDtypeStruct((slots, LS, BLOCK), F32),
            jax.ShapeDtypeStruct((LS, LANES), F32),
        ),
        in_specs=[smem_spec()] + [vmem_spec()] * 4,
        out_specs=(vmem_spec(),) * 3,
        compiler_params=params(8),
        name="combine",
    )(meta, loc, own_one, fwd_one, got_one)
    far_w = lax.all_to_all(send_w, "col", split_axis=0, concat_axis=0, tiled=True)
    own_two = own(w, False)
    fwd_two, back_two = pl.pallas_call(
        second_kernel,
        out_shape=(field, jax.ShapeDtypeStruct((cols, CAP * LS, BLOCK + LANES), F32)),
        in_specs=[hbm_spec(), smem_spec()] + [vmem_spec()] * 4 + [any_spec()] * 3,
        out_specs=(vmem_spec(),) * 2,
        scratch_shapes=[
            SMEM((most,), jnp.int32),
            VMEM((3, BLOCK, LANES), F32),
            VMEM((count, LS, BLOCK, LANES), F32),
            VMEM((BLOCK, BLOCK), F32),
            VMEM((count, LS, BLOCK, LANES), F32),
            VMEM((LS, BLOCK), F32),
            VMEM((LS, BLOCK), F32),
            VMEM((8, BLOCK, BLOCK), BF16),
            VMEM((slots, LS, BLOCK), F32),
            VMEM((slots, LS, BLOCK), F32),
            SMEM((LS,), F32),
            pltpu.SemaphoreType.DMA((8,)),
            pltpu.SemaphoreType.DMA((3,)),
        ],
        compiler_params=params(40),
        cost_estimate=pl.CostEstimate(flops=5 * 10**9, bytes_accessed=6 * 10**7, transcendentals=0),
        name="cross_second",
    )(lengthscales, meta, loc, w, own_two, dots_one, far, far_w, tiles)
    got_two = lax.all_to_all(back_two, "col", split_axis=0, concat_axis=0, tiled=True)

    dots_two = pl.pallas_call(
        dots_kernel,
        out_shape=jax.ShapeDtypeStruct((rows, LANES), F32),
        in_specs=[pl.BlockSpec((cols, LS, LANES), lambda i: (0, 0, BLOCK // LANES))],
        out_specs=pl.BlockSpec((rows, LANES), lambda i: (0, 0)),
        grid=(1,),
        compiler_params=params(4),
        name="dots",
    )(got_two)
    dots = lax.all_to_all(dots_two, "row", split_axis=0, concat_axis=0, tiled=True)
    z = pl.pallas_call(
        gather_kernel,
        out_shape=field,
        in_specs=[smem_spec()] + [vmem_spec()] * 2,
        out_specs=vmem_spec(),
        compiler_params=params(8),
        cost_estimate=pl.CostEstimate(flops=10**8, bytes_accessed=2 * 10**6, transcendentals=0),
        name="gather",
    )(meta, fwd_two, got_two)
    return pl.pallas_call(
        finish_kernel,
        out_shape=(jax.ShapeDtypeStruct((LS, total), F32),) * 2,
        in_specs=[smem_spec()] + [vmem_spec()] * 4,
        out_specs=(vmem_spec(),) * 2,
        compiler_params=params(8),
        name="finish",
    )(noise_level, loc, w, z, dots)


def solution(mesh):
    placed = (P(None, ("row", "col")), P(("row", "col")), P(("row", "col")), P(), P(), P(), P())
    return jax.shard_map(
        on_device,
        mesh=mesh,
        in_specs=placed,
        out_specs=(P(None, ("row", "col")), P(None, ("row", "col"))),
        check_vma=False,
    )
```

```python
import jax
import jax.numpy as jnp
from jax import lax
from jax.experimental import pallas as pl
from jax.experimental.pallas import tpu as pltpu
from jax.sharding import PartitionSpec as P

BLOCK = 512
LS = 8
CAP = 2
LANES = 128
CHUNK = 16
DOTS = 5
APART = 2
F32 = jnp.float32
BF16 = jnp.bfloat16
VMEM = pltpu.VMEM
SMEM = pltpu.SMEM


def vmem_spec():
    return pl.BlockSpec(memory_space=pltpu.VMEM)


def smem_spec():
    return pl.BlockSpec(memory_space=pltpu.SMEM)


def any_spec():
    return pl.BlockSpec(memory_space=pl.ANY)


def hbm_spec():
    return pl.BlockSpec(memory_space=pltpu.HBM)


def start_copies(sources, targets, sems):
    copies = [pltpu.make_async_copy(a, b, sems.at[n]) for n, (a, b) in enumerate(zip(sources, targets))]
    for copy in copies:
        copy.start()
    return copies


def params(mebibytes):
    return pltpu.CompilerParams(vmem_limit_bytes=mebibytes * 2**20)


def over(value, size):
    return value >> (size.bit_length() - 1) if size & (size - 1) == 0 else value // size


def rest(value, size):
    return value & (size - 1) if size & (size - 1) == 0 else value % size


def order_kernel(scale_ref, pts_hbm, tgt_hbm, order_hbm, loc_ref, send_ref, slope_ref, pts_ref, tgt_ref, order_ref, sems):
    for copy in start_copies((pts_hbm, tgt_hbm, order_hbm), (pts_ref, tgt_ref, order_ref), sems):
        copy.wait()
    slope_ref[...] = CREST / per_system(scale_ref)
    total = pts_ref.shape[1]
    pieces = total // LANES
    per = BLOCK // LANES
    source = jnp.concatenate([pts_ref[...], tgt_ref[...], jnp.zeros((4, total), F32)], axis=0)
    for o in range(pieces):
        index = jnp.broadcast_to(order_ref[:, o * LANES:(o + 1) * LANES], (8, LANES))
        high = over(index, LANES)
        low = rest(index, LANES)
        got = jnp.zeros((8, LANES), F32)
        for c in range(pieces):
            part = jnp.take_along_axis(
                source[:, c * LANES:(c + 1) * LANES], low, axis=1, mode="promise_in_bounds"
            )
            got = jnp.where(high == c, part, got)
        loc_ref[o // per, :, (o % per) * LANES:(o % per + 1) * LANES] = got
    halves = []
    for h in range(loc_ref.shape[0] // 2):
        halves.append(jnp.concatenate([loc_ref[2 * h, 0:4, :], loc_ref[2 * h + 1, 0:4, :]], axis=0))
    for c in range(send_ref.shape[0] // len(halves)):
        for h in range(len(halves)):
            send_ref[c * len(halves) + h] = halves[h]


SPARE = 63


def plan_kernel(cols, count, pairs_dev, me_ref, owner_hbm, pairs_hbm, meta_ref, peer_ref, cost_ref, turn_ref, load_ref, have_ref, asking_ref, used_ref, owner_ref, pairs_ref, sems):
    copies = start_copies((owner_hbm, pairs_hbm), (owner_ref, pairs_ref), sems)
    mine = rest(me_ref[0], cols)
    start = over(me_ref[0], cols) * (cols * pairs_dev)

    def clear(i, _):
        for c in range(cols):
            have_ref[i * cols + c] = 0
        for c in range(4):
            used_ref[c * cols + i] = 0
        return 0

    lax.fori_loop(0, cols, clear, 0)
    for q in range(cols * CAP):
        meta_ref[4, q] = -1
    for copy in copies:
        copy.wait()

    def read(d, asking):
        total = jnp.int32(0)
        for j in range(pairs_dev):
            p = d * pairs_dev + j
            e = rest(over(owner_ref[pairs_ref[1, start + p]], count), cols)
            cost = 4 * (LS - pairs_ref[2, start + p]) + 3
            peer_ref[p] = e
            cost_ref[p] = cost
            total = total + cost
            have_ref[d * cols + e] = have_ref[d * cols + e] + 1
            asking_ref[asking] = p
            asking = asking + (e == mine).astype(jnp.int32)
        load_ref[d] = total
        return asking

    asking = lax.fori_loop(0, cols, read, jnp.int32(0))

    def weigh(j, _):
        for d in range(cols):
            p = d * pairs_dev + j
            e = peer_ref[p]
            cost = cost_ref[p]
            here = load_ref[d]
            there = load_ref[e]
            back = have_ref[e * cols + d]
            turn = jnp.logical_and(here - there > cost, back < CAP).astype(jnp.int32)
            load_ref[d] = here - turn * cost
            load_ref[e] = there + turn * cost
            have_ref[e * cols + d] = back + turn
            turn_ref[p] = turn
        return 0

    lax.fori_loop(0, pairs_dev, weigh, 0)

    def lay(p, other, here, number):
        turn = turn_ref[p]
        turned = turn == 1
        near = rest(owner_ref[pairs_ref[0, start + p]], count)
        far = rest(owner_ref[pairs_ref[1, start + p]], count)
        at_used = (2 * here + turn) * cols + other
        seen = used_ref[at_used]
        used_ref[at_used] = seen + 1
        slot = other * CAP + jnp.where(turned, CAP - 1 - seen, seen)
        ours = turn == here
        mine_block, their_block = (far, near) if here else (near, far)
        at = jnp.where(ours, number, SPARE)
        meta_ref[0, at] = mine_block
        meta_ref[1, at] = slot
        meta_ref[2, at] = pairs_ref[2, start + p]
        meta_ref[3, at] = other * count + their_block
        meta_ref[4, jnp.where(ours, SPARE, slot)] = mine_block
        return number + ours.astype(jnp.int32)

    number = jnp.int32(0)
    for j in range(pairs_dev):
        p = mine * pairs_dev + j
        number = lay(p, peer_ref[p], 0, number)

    def lay_asking(i, number):
        p = asking_ref[i]
        return lay(p, over(p, pairs_dev), 1, number)

    meta_ref[5, 0] = lax.fori_loop(0, asking, lay_asking, number)


def spread_columns(rows):
    turned = jnp.transpose(rows)
    return [jnp.broadcast_to(turned[:, k:k + 1], (BLOCK, LANES)) for k in range(8)]


def rounded(values):
    return values.astype(BF16).astype(F32)


def per_system(ref):
    which = lax.broadcasted_iota(jnp.int32, (LS, LANES), 0)
    out = jnp.zeros((LS, LANES), F32)
    for l in range(LS):
        out = jnp.where(which == l, ref[l], out)
    return out


def wide(column, width):
    return jnp.concatenate([column] * (width // LANES), axis=1)


def lane_fold(values):
    total = values[:, 0:LANES]
    for c in range(1, values.shape[1] // LANES):
        total = total + values[:, c * LANES:(c + 1) * LANES]
    return total


def distance(col_refs, row_vals, width):
    summed = None
    for k in range(3):
        differ = wide(col_refs[k], width) - row_vals[k]
        square = differ * differ
        summed = square if summed is None else summed + square
    summed = jnp.maximum(summed, 1e-30)
    return summed * lax.rsqrt(summed)


CREST = 4.0**0.2


def slope_of(slope_ref, l):
    return jnp.broadcast_to(slope_ref[pl.ds(l, 1), :], (CHUNK, LANES))


def kernel_value(dist, slope):
    remain = jnp.maximum(CREST - dist * wide(slope, dist.shape[1]), 0.0)
    squared = remain * remain
    return ((squared * squared) * (5.0 / CREST**4 - remain)).astype(BF16)


def sub_fold(values):
    return values[0:8, :] + values[8:16, :]


def fold_forward(forward_ref, s):
    lane = lax.broadcasted_iota(jnp.int32, (LANES, LANES), 1)
    out = []
    for part in range(BLOCK // LANES):
        held = jnp.zeros((LANES, LANES), F32)
        for l in range(LS):
            block = forward_ref[s, l, part * LANES:(part + 1) * LANES, :]
            held = jnp.where(lane == l, jnp.sum(block, axis=1, keepdims=True), held)
        out.append(jnp.transpose(held)[0:LS, :])
    return jnp.concatenate(out, axis=1)


def partner_rows(far_ref, which):
    both = far_ref[over(which, 2)]
    return jnp.where(rest(which, 2) == 1, both[4:8, :], both[0:4, :])


def own_tiles(common, s, ls_ref, loc_ref, vec_ref, coord_ref, col_ref, dist_ref, forward_ref, out_ref):
    parts = BLOCK // LANES
    per = LANES // CHUNK
    turns = LS // 2
    for part in range(parts):
        low = part * LANES
        width = BLOCK - low
        rows = [loc_ref[s, k:k + 1, low:] for k in range(3)]

        def measure(c, _):
            at = pl.ds(pl.multiple_of(low + c * CHUNK, CHUNK), CHUNK)
            dist_ref[at, low:] = distance([coord_ref[k, at, :] for k in range(3)], rows, width)
            return 0

        lax.fori_loop(0, per, measure, 0, unroll=8)

    def two(t, _):
        back = [jnp.zeros((8, BLOCK), F32) for _ in range(2)]
        ids = [2 * t, 2 * t + 1]
        slopes = [slope_of(ls_ref, l) for l in ids]
        for part in range(parts):
            low = part * LANES
            width = BLOCK - low
            if common:
                rows = [rounded(loc_ref[s, 3:4, low:])] * 2
            else:
                rows = [vec_ref[s, pl.ds(l, 1), :][:, low:] for l in ids]

            def step(c, held):
                at = slice(low + c * CHUNK, low + (c + 1) * CHUNK)
                dist = dist_ref[at, low:]
                fresh = []
                for n in range(2):
                    value = kernel_value(dist, slopes[n]).astype(F32)
                    forward_ref[ids[n], at, :] = lane_fold(value * rows[n])
                    if width > LANES:
                        column = coord_ref[3, at, :] if common else col_ref[ids[n], at, :]
                        right = value[:, LANES:] * wide(column, width - LANES)
                        fresh.append(held[n] + sub_fold(right))
                return tuple(fresh) if fresh else held

            start = max(width - LANES, LANES)
            held = tuple(jnp.zeros((8, start), F32) for _ in range(2))
            for c in range(per):
                held = step(c, held)
            if width > LANES:
                for n in range(2):
                    back[n] = jnp.concatenate(
                        [back[n][:, :low + LANES], back[n][:, low + LANES:] + held[n]], axis=1
                    )
        for n in range(2):
            out_ref[pl.ds(ids[n], 1), :] = jnp.sum(back[n], axis=0, keepdims=True)
        return 0

    lax.fori_loop(0, turns, two, 0)


def own_kernel(common, ls_ref, loc_ref, vec_ref, out_ref, coord_ref, col_ref, dist_ref, forward_ref):
    def block(s, _):
        columns = spread_columns(loc_ref[s])
        for k in range(4):
            coord_ref[k] = columns[k]
        if common:
            coord_ref[3] = rounded(columns[3])
        else:
            columns = spread_columns(vec_ref[s])
            for l in range(LS):
                col_ref[l] = columns[l]
        own_tiles(
            common, s, ls_ref, loc_ref, vec_ref, coord_ref, col_ref, dist_ref, forward_ref.at[0], out_ref.at[s]
        )
        out_ref[s] = out_ref[s] + fold_forward(forward_ref, 0)
        return 0

    lax.fori_loop(0, APART, block, 0)


def first_kernel(
    ls_ref, meta_ref, loc_ref, far_hbm_ref,
    out_ref, back_ref, tiles_ref,
    coord_ref, dist_ref, forward_ref, stage_ref, far_ref, sem_ref, far_sem,
):
    count = loc_ref.shape[0]
    pair_count = meta_ref[5, 0]
    steps = BLOCK // CHUNK
    (far_copy,) = start_copies((far_hbm_ref,), (far_ref,), far_sem)
    for s in range(count):
        columns = spread_columns(loc_ref[s])
        for k in range(3):
            coord_ref[s, k] = columns[k]
        coord_ref[s, 3] = rounded(columns[3])
    for s in range(APART):
        forward_ref[s] = jnp.zeros(forward_ref.shape[1:], F32)
        out_ref[s] = jnp.zeros(out_ref.shape[1:], F32)

    def own(s, _):
        own_tiles(
            True, s, ls_ref, loc_ref, None, coord_ref.at[s], None, dist_ref, forward_ref.at[s], out_ref.at[s]
        )
        return 0

    lax.fori_loop(APART, count, own, 0)
    far_copy.wait()

    def store_copy(slot, number):
        return pltpu.make_async_copy(stage_ref.at[slot], tiles_ref.at[number], sem_ref.at[slot])

    def pair(p, number):
        a = meta_ref[0, p]
        q = meta_ref[1, p]
        reach = meta_ref[2, p]
        mine = partner_rows(far_ref, meta_ref[3, p])
        rows = [mine[k:k + 1, :] for k in range(3)]
        values = rounded(mine[3:4, :])

        def measure(c, _):
            at = pl.ds(pl.multiple_of(c * CHUNK, CHUNK), CHUNK)
            dist_ref[at, :] = distance([coord_ref[a, k, at, :] for k in range(3)], rows, BLOCK)
            return 0

        lax.fori_loop(0, steps, measure, 0, unroll=8)
        back_ref[q] = jnp.zeros((LS, BLOCK), F32)

        def sweep(ids, number):
            slopes = [slope_of(ls_ref, l) for l in ids]
            slots = [(number + n) % 4 for n in range(len(ids))]
            for n in range(len(ids)):
                @pl.when(number + n >= 4)
                def _():
                    store_copy(slots[n], number + n).wait()

            def step(c, held):
                at = pl.ds(pl.multiple_of(c * CHUNK, CHUNK), CHUNK)
                dist = dist_ref[at, :]
                column = wide(coord_ref[a, 3, at, :], BLOCK)
                fresh = []
                for n in range(len(ids)):
                    value = kernel_value(dist, slopes[n])
                    stage_ref[slots[n], at, :] = value
                    value = value.astype(F32)
                    forward_ref[a, ids[n], at, :] += lane_fold(value * values)
                    fresh.append(held[n] + sub_fold(value * column))
                return tuple(fresh)

            held = tuple(jnp.zeros((8, BLOCK), F32) for _ in ids)
            held = lax.fori_loop(0, steps, step, held, unroll=8)
            for n in range(len(ids)):
                back_ref[q, pl.ds(ids[n], 1), :] = jnp.sum(held[n], axis=0, keepdims=True)
                store_copy(slots[n], number + n).start()
            return number + len(ids)

        live = LS - reach

        def two(t, number):
            return sweep([LS - 1 - 2 * t, LS - 2 - 2 * t], number)

        number = lax.fori_loop(0, live // 2, two, number)
        return lax.cond(live % 2 == 1, lambda m: sweep([reach], m), lambda m: m, number)

    number = lax.fori_loop(0, pair_count, pair, jnp.int32(0))
    for back in range(4):
        @pl.when(number > back)
        def _():
            store_copy((number - 1 - back) % 4, number - 1 - back).wait()

    for s in range(count):
        out_ref[s] = out_ref[s] + fold_forward(forward_ref, s)


def combine_kernel(
    meta_ref, loc_ref, own_ref, fwd_ref, got_ref, w_ref, send_ref, dots_ref
):
    count = loc_ref.shape[0]
    slots = got_ref.shape[0]
    w_ref[...] = fwd_ref[...]
    for s in range(APART):
        w_ref[s] = w_ref[s] + own_ref[s]
    for q in range(slots):
        where = meta_ref[4, q]

        @pl.when(where >= 0)
        def _():
            w_ref[where] = w_ref[where] + got_ref[q]

    unit = 1.0 / (2.0 * BLOCK)
    products = [jnp.zeros((LS, BLOCK), F32) for _ in range(3)]
    for s in range(count):
        value = w_ref[s] * unit
        w_ref[s] = value
        target = jnp.broadcast_to(loc_ref[s, 3:4, :], (LS, BLOCK))
        products[0] = products[0] + target * target
        products[1] = products[1] + target * value
        products[2] = products[2] + value * value
    for q in range(slots):
        send_ref[q] = w_ref[jnp.maximum(meta_ref[4, q], 0)]
    lane = lax.broadcasted_iota(jnp.int32, (LS, LANES), 1)
    held = jnp.zeros((LS, LANES), F32)
    for n in range(3):
        held = jnp.where(lane == n, jnp.sum(products[n], axis=1, keepdims=True), held)
    dots_ref[...] = held


def second_kernel(
    ls_ref, meta_ref, loc_ref, w_ref, own_ref, dots_ref, far_pts_hbm_ref, far_hbm_ref, tiles_ref,
    out_ref, back_ref,
    list_ref, coord_ref, col_ref, dist_ref, forward_ref, wz_ref, yz_ref, stage_ref, far_pts_ref, far_ref,
    sem_ref, far_sem,
):
    count = w_ref.shape[0]
    pair_count = meta_ref[5, 0]
    steps = BLOCK // CHUNK
    depth = stage_ref.shape[0]
    copies = start_copies((far_pts_hbm_ref, far_hbm_ref), (far_pts_ref, far_ref), far_sem)

    def list_pair(p, number):
        reach = meta_ref[2, p]
        live = LS - reach

        def two(t, number):
            list_ref[number] = p * LS + LS - 1 - t
            return number + 1

        return lax.fori_loop(0, live, two, number)

    number = lax.fori_loop(0, pair_count, list_pair, jnp.int32(0))

    def load_copy(t):
        slot = t % depth
        return pltpu.make_async_copy(tiles_ref.at[t], stage_ref.at[slot], sem_ref.at[slot])

    for t in range(depth - 1):
        @pl.when(t < number)
        def _():
            load_copy(jnp.int32(t)).start()


    def clear(p, _):
        q = meta_ref[1, p]
        back_ref[over(q, CAP), pl.ds(pl.multiple_of(rest(q, CAP) * LS, LS), LS), :BLOCK] = jnp.zeros((LS, BLOCK), F32)
        return 0

    lax.fori_loop(0, pair_count, clear, 0)
    for s in range(count):
        columns = spread_columns(w_ref[s])
        for l in range(LS):
            col_ref[s, l] = columns[l]
    for s in range(APART):
        forward_ref[s] = jnp.zeros(forward_ref.shape[1:], F32)
        out_ref[s] = own_ref[s]

    def own(s, _):
        columns = spread_columns(loc_ref[s])
        for k in range(3):
            coord_ref[k] = columns[k]
        own_tiles(
            False, s, ls_ref, loc_ref, w_ref, coord_ref, col_ref.at[s], dist_ref, forward_ref.at[s], out_ref.at[s]
        )
        return 0

    lax.fori_loop(APART, count, own, 0)
    for copy in copies:
        copy.wait()
    wz_ref[...] = jnp.zeros(wz_ref.shape, F32)
    yz_ref[...] = jnp.zeros(yz_ref.shape, F32)

    def tile(t, _):
        entry = list_ref[t]
        p = over(entry, LS)
        l = rest(entry, LS)
        a = meta_ref[0, p]
        q = meta_ref[1, p]
        slot = t % depth

        @pl.when(t + depth - 1 < number)
        def _():
            load_copy(t + depth - 1).start()

        load_copy(t).wait()
        row = far_ref[q, pl.ds(l, 1), :]

        def step(c, held):
            at = pl.ds(pl.multiple_of(c * CHUNK, CHUNK), CHUNK)
            value = stage_ref[slot, at, :].astype(F32)
            forward_ref[a, l, at, :] += lane_fold(value * row)
            return held + sub_fold(value * wide(col_ref[a, l, at, :], BLOCK))

        held = lax.fori_loop(0, steps, step, jnp.zeros((8, BLOCK), F32), unroll=32)
        result = jnp.sum(held, axis=0, keepdims=True)
        back_ref[over(q, CAP), pl.ds(rest(q, CAP) * LS + l, 1), :BLOCK] = result
        target = partner_rows(far_pts_ref, meta_ref[3, p])[3:4, :]
        wz_ref[pl.ds(l, 1), :] += result * row
        yz_ref[pl.ds(l, 1), :] += result * target
        return 0

    lax.fori_loop(0, number, tile, 0)
    wz = wz_ref[...]
    yz = yz_ref[...]
    for s in range(count):
        value = out_ref[s] + fold_forward(forward_ref, s)
        out_ref[s] = value
        wz = wz + value * w_ref[s]
        yz = yz + value * loc_ref[s, 3:4, :]
    unit = 1.0 / (2.0 * BLOCK)
    lane = lax.broadcasted_iota(jnp.int32, (LS, LANES), 1)
    held = jnp.where(lane == 3, jnp.sum(wz, axis=1, keepdims=True) * unit, dots_ref[...])
    held = jnp.where(lane == 4, jnp.sum(yz, axis=1, keepdims=True) * unit, held)
    for c in range(back_ref.shape[0]):
        back_ref[c, 0:LS, BLOCK:] = held


SPAN = LANES // LS


def system_lanes(n):
    sub = lax.broadcasted_iota(jnp.int32, (LS, LANES), 0)
    lane = lax.broadcasted_iota(jnp.int32, (LS, LANES), 1)
    return lane == sub * SPAN + n


def dots_kernel(got_ref, dots_ref):
    held = got_ref[0, 0:LS, :]
    for c in range(1, got_ref.shape[0]):
        held = held + got_ref[c, 0:LS, :]
    row = jnp.zeros((LS, LANES), F32)
    for n in range(DOTS):
        row = jnp.where(system_lanes(n), held[:, n:n + 1], row)
    row = jnp.sum(row, axis=0, keepdims=True)
    dots_ref[...] = jnp.broadcast_to(row, dots_ref.shape)


def gather_kernel(meta_ref, part_ref, got_ref, z_ref):
    z_ref[...] = part_ref[...]
    for c in range(got_ref.shape[0]):
        for k in range(CAP):
            where = meta_ref[4, c * CAP + k]

            @pl.when(where >= 0)
            def _():
                z_ref[where] = z_ref[where] + got_ref[c, k * LS:(k + 1) * LS, :BLOCK]

    z_ref[...] = z_ref[...] * (1.0 / (2.0 * BLOCK))


def finish_kernel(noise_ref, loc_ref, w_ref, z_ref, dots_ref, sol_ref, res_ref):
    row = jnp.sum(dots_ref[...], axis=0, keepdims=True)
    spread = jnp.broadcast_to(row, (LS, LANES))
    noise = per_system(noise_ref)[:, 0:1]
    yy, yw, ww, wz, yz = [
        jnp.sum(jnp.where(system_lanes(n), spread, 0.0), axis=1, keepdims=True) for n in range(DOTS)
    ]
    curve = noise * yy + yw
    first = yy / curve
    keep = yw / curve
    fresh = first * ((yy * ww - yw * yw) / curve)
    beta = fresh / yy
    gain = keep + beta
    bend = noise * fresh * (1.0 + beta) + gain * gain * yw - gain * first * (ww + yz) + first * first * wz
    second = fresh / bend
    sol_y = first + second * gain
    sol_w = second * first
    res_y = keep - second * noise * gain
    res_w = second * (noise * first - gain) - first
    for s in range(loc_ref.shape[0]):
        target = loc_ref[s, 3:4, :]
        value = w_ref[s]
        sol_ref[:, s * BLOCK:(s + 1) * BLOCK] = sol_y * target - sol_w * value
        res_ref[:, s * BLOCK:(s + 1) * BLOCK] = res_y * target + res_w * value + sol_w * z_ref[s]


def on_device(points, targets, kd_order, lengthscales, noise_level, block_owner, block_pairs):
    cols = lax.axis_size("col")
    rows = lax.axis_size("row")
    me = (lax.axis_index("row") * cols + lax.axis_index("col")).astype(jnp.int32).reshape(1)
    total = points.shape[1]
    count = total // BLOCK
    pairs_dev = block_pairs.shape[1] // (rows * cols)
    slots = cols * CAP
    most = (cols - 1) * CAP * LS
    field = jax.ShapeDtypeStruct((count, LS, BLOCK), F32)

    loc, send, slopes = pl.pallas_call(
        order_kernel,
        out_shape=(
            jax.ShapeDtypeStruct((count, 8, BLOCK), F32),
            jax.ShapeDtypeStruct((cols * (count // 2), 8, BLOCK), F32),
            jax.ShapeDtypeStruct((LS, LANES), F32),
        ),
        in_specs=[smem_spec()] + [hbm_spec()] * 3,
        out_specs=(vmem_spec(),) * 3,
        scratch_shapes=[
            VMEM((3, total), F32),
            VMEM((1, total), F32),
            VMEM((1, total), jnp.int32),
            pltpu.SemaphoreType.DMA((3,)),
        ],
        compiler_params=params(8),
        name="order",
    )(lengthscales, points, targets.reshape(1, total), kd_order.reshape(1, total))
    def own(vec, common):
        return pl.pallas_call(
            lambda *refs: own_kernel(common, *refs),
            out_shape=jax.ShapeDtypeStruct((APART, LS, BLOCK), F32),
            in_specs=[vmem_spec(), vmem_spec(), vmem_spec()],
            out_specs=vmem_spec(),
            scratch_shapes=[
                VMEM((4, BLOCK, LANES), F32),
                VMEM((LS, BLOCK, LANES), F32),
                VMEM((BLOCK, BLOCK), F32),
                VMEM((1, LS, BLOCK, LANES), F32),
            ],
            compiler_params=params(16),
            cost_estimate=pl.CostEstimate(flops=2 * 10**9, bytes_accessed=10**6, transcendentals=0),
            name="own_first" if common else "own_second",
        )(slopes, loc, vec)

    far = lax.all_to_all(send, "col", split_axis=0, concat_axis=0, tiled=True)
    meta = pl.pallas_call(
        lambda *refs: plan_kernel(cols, count, pairs_dev, *refs),
        out_shape=jax.ShapeDtypeStruct((8, SPARE + 1), jnp.int32),
        in_specs=[smem_spec(), hbm_spec(), hbm_spec()],
        out_specs=smem_spec(),
        scratch_shapes=[
            SMEM((n,), jnp.int32)
            for n in [cols * pairs_dev] * 3 + [cols, cols * cols, cols * pairs_dev + 1, 4 * cols]
        ] + [
            SMEM(block_owner.shape, jnp.int32),
            SMEM(block_pairs.shape, jnp.int32),
            pltpu.SemaphoreType.DMA((2,)),
        ],
        compiler_params=params(8),
        cost_estimate=pl.CostEstimate(flops=10**9, bytes_accessed=10**6, transcendentals=0),
        name="plan",
    )(me, block_owner, block_pairs)
    own_one = own(loc, True)
    fwd_one, back_one, tiles = pl.pallas_call(
        first_kernel,
        out_shape=(
            field,
            jax.ShapeDtypeStruct((slots, LS, BLOCK), F32),
            jax.ShapeDtypeStruct((most, BLOCK, BLOCK), BF16),
        ),
        in_specs=[vmem_spec(), smem_spec(), vmem_spec(), any_spec()],
        out_specs=(vmem_spec(), vmem_spec(), any_spec()),
        scratch_shapes=[
            VMEM((count, 4, BLOCK, LANES), F32),
            VMEM((BLOCK, BLOCK), F32),
            VMEM((count, LS, BLOCK, LANES), F32),
            VMEM((4, BLOCK, BLOCK), BF16),
            VMEM((slots, LS, BLOCK), F32),
            pltpu.SemaphoreType.DMA((4,)),
            pltpu.SemaphoreType.DMA((1,)),
        ],
        compiler_params=params(28),
        cost_estimate=pl.CostEstimate(flops=10**10, bytes_accessed=6 * 10**7, transcendentals=0),
        name="cross_first",
    )(slopes, meta, loc, far)
    got_one = lax.all_to_all(back_one, "col", split_axis=0, concat_axis=0, tiled=True)

    w, send_w, dots_one = pl.pallas_call(
        combine_kernel,
        out_shape=(
            field,
            jax.ShapeDtypeStruct((slots, LS, BLOCK), F32),
            jax.ShapeDtypeStruct((LS, LANES), F32),
        ),
        in_specs=[smem_spec()] + [vmem_spec()] * 4,
        out_specs=(vmem_spec(),) * 3,
        compiler_params=params(8),
        name="combine",
    )(meta, loc, own_one, fwd_one, got_one)
    far_w = lax.all_to_all(send_w, "col", split_axis=0, concat_axis=0, tiled=True)
    own_two = own(w, False)
    fwd_two, back_two = pl.pallas_call(
        second_kernel,
        out_shape=(field, jax.ShapeDtypeStruct((cols, CAP * LS, BLOCK + LANES), F32)),
        in_specs=[vmem_spec(), smem_spec()] + [vmem_spec()] * 4 + [any_spec()] * 3,
        out_specs=(vmem_spec(),) * 2,
        scratch_shapes=[
            SMEM((most,), jnp.int32),
            VMEM((3, BLOCK, LANES), F32),
            VMEM((count, LS, BLOCK, LANES), F32),
            VMEM((BLOCK, BLOCK), F32),
            VMEM((count, LS, BLOCK, LANES), F32),
            VMEM((LS, BLOCK), F32),
            VMEM((LS, BLOCK), F32),
            VMEM((8, BLOCK, BLOCK), BF16),
            VMEM((slots, LS, BLOCK), F32),
            VMEM((slots, LS, BLOCK), F32),
            pltpu.SemaphoreType.DMA((8,)),
            pltpu.SemaphoreType.DMA((2,)),
        ],
        compiler_params=params(40),
        cost_estimate=pl.CostEstimate(flops=5 * 10**9, bytes_accessed=6 * 10**7, transcendentals=0),
        name="cross_second",
    )(slopes, meta, loc, w, own_two, dots_one, far, far_w, tiles)
    got_two = lax.all_to_all(back_two, "col", split_axis=0, concat_axis=0, tiled=True)

    dots_two = pl.pallas_call(
        dots_kernel,
        out_shape=jax.ShapeDtypeStruct((rows, LANES), F32),
        in_specs=[pl.BlockSpec((cols, LS, LANES), lambda i: (0, 0, BLOCK // LANES))],
        out_specs=pl.BlockSpec((rows, LANES), lambda i: (0, 0)),
        grid=(1,),
        compiler_params=params(4),
        name="dots",
    )(got_two)
    dots = lax.all_to_all(dots_two, "row", split_axis=0, concat_axis=0, tiled=True)
    z = pl.pallas_call(
        gather_kernel,
        out_shape=field,
        in_specs=[smem_spec()] + [vmem_spec()] * 2,
        out_specs=vmem_spec(),
        compiler_params=params(8),
        cost_estimate=pl.CostEstimate(flops=10**8, bytes_accessed=2 * 10**6, transcendentals=0),
        name="gather",
    )(meta, fwd_two, got_two)
    return pl.pallas_call(
        finish_kernel,
        out_shape=(jax.ShapeDtypeStruct((LS, total), F32),) * 2,
        in_specs=[smem_spec()] + [vmem_spec()] * 4,
        out_specs=(vmem_spec(),) * 2,
        compiler_params=params(8),
        name="finish",
    )(noise_level, loc, w, z, dots)


def solution(mesh):
    placed = (P(None, ("row", "col")), P(("row", "col")), P(("row", "col")), P(), P(), P(), P())
    return jax.shard_map(
        on_device,
        mesh=mesh,
        in_specs=placed,
        out_specs=(P(None, ("row", "col")), P(None, ("row", "col"))),
        check_vma=False,
    )
```

```python
import jax
import jax.numpy as jnp
from jax import lax
from jax.experimental import pallas as pl
from jax.experimental.pallas import tpu as pltpu
from jax.sharding import PartitionSpec as P

BLOCK = 512
LS = 8
CAP = 2
LANES = 128
CHUNK = 16
DOTS = 5
APART = 2
F32 = jnp.float32
BF16 = jnp.bfloat16
VMEM = pltpu.VMEM
SMEM = pltpu.SMEM


def vmem_spec():
    return pl.BlockSpec(memory_space=pltpu.VMEM)


def smem_spec():
    return pl.BlockSpec(memory_space=pltpu.SMEM)


def any_spec():
    return pl.BlockSpec(memory_space=pl.ANY)


def hbm_spec():
    return pl.BlockSpec(memory_space=pltpu.HBM)


def start_copies(sources, targets, sems):
    copies = [pltpu.make_async_copy(a, b, sems.at[n]) for n, (a, b) in enumerate(zip(sources, targets))]
    for copy in copies:
        copy.start()
    return copies


def params(mebibytes):
    return pltpu.CompilerParams(vmem_limit_bytes=mebibytes * 2**20)


def over(value, size):
    return value >> (size.bit_length() - 1) if size & (size - 1) == 0 else value // size


def rest(value, size):
    return value & (size - 1) if size & (size - 1) == 0 else value % size


def order_kernel(scale_ref, pts_hbm, tgt_hbm, order_hbm, loc_ref, send_ref, slope_ref, pts_ref, tgt_ref, order_ref, sems):
    for copy in start_copies((pts_hbm, tgt_hbm, order_hbm), (pts_ref, tgt_ref, order_ref), sems):
        copy.wait()
    slope_ref[...] = CREST / per_system(scale_ref)
    total = pts_ref.shape[1]
    pieces = total // LANES
    per = BLOCK // LANES
    source = jnp.concatenate([pts_ref[...], tgt_ref[...], jnp.zeros((4, total), F32)], axis=0)
    for o in range(pieces):
        index = jnp.broadcast_to(order_ref[:, o * LANES:(o + 1) * LANES], (8, LANES))
        high = over(index, LANES)
        low = rest(index, LANES)
        got = jnp.zeros((8, LANES), F32)
        for c in range(pieces):
            part = jnp.take_along_axis(
                source[:, c * LANES:(c + 1) * LANES], low, axis=1, mode="promise_in_bounds"
            )
            got = jnp.where(high == c, part, got)
        loc_ref[o // per, :, (o % per) * LANES:(o % per + 1) * LANES] = got
    halves = []
    for h in range(loc_ref.shape[0] // 2):
        halves.append(jnp.concatenate([loc_ref[2 * h, 0:4, :], loc_ref[2 * h + 1, 0:4, :]], axis=0))
    for c in range(send_ref.shape[0] // len(halves)):
        for h in range(len(halves)):
            send_ref[c * len(halves) + h] = halves[h]


SPARE = 63


def plan_kernel(cols, count, pairs_dev, me_ref, owner_hbm, pairs_hbm, meta_ref, peer_ref, cost_ref, turn_ref, load_ref, have_ref, asking_ref, used_ref, owner_ref, pairs_ref, sems):
    copies = start_copies((owner_hbm, pairs_hbm), (owner_ref, pairs_ref), sems)
    mine = rest(me_ref[0], cols)
    start = over(me_ref[0], cols) * (cols * pairs_dev)

    def clear(i, _):
        for c in range(cols):
            have_ref[i * cols + c] = 0
        for c in range(4):
            used_ref[c * cols + i] = 0
        return 0

    lax.fori_loop(0, cols, clear, 0)
    for q in range(cols * CAP):
        meta_ref[4, q] = -1
    for copy in copies:
        copy.wait()

    def read(d, asking):
        total = jnp.int32(0)
        for j in range(pairs_dev):
            p = d * pairs_dev + j
            e = rest(over(owner_ref[pairs_ref[1, start + p]], count), cols)
            cost = 4 * (LS - pairs_ref[2, start + p]) + 3
            peer_ref[p] = e
            cost_ref[p] = cost
            total = total + cost
            have_ref[d * cols + e] = have_ref[d * cols + e] + 1
            asking_ref[asking] = p
            asking = asking + (e == mine).astype(jnp.int32)
        load_ref[d] = total
        return asking

    asking = lax.fori_loop(0, cols, read, jnp.int32(0))

    def weigh(j, _):
        for d in range(cols):
            p = d * pairs_dev + j
            e = peer_ref[p]
            cost = cost_ref[p]
            here = load_ref[d]
            there = load_ref[e]
            back = have_ref[e * cols + d]
            turn = jnp.logical_and(here - there > cost, back < CAP).astype(jnp.int32)
            load_ref[d] = here - turn * cost
            load_ref[e] = there + turn * cost
            have_ref[e * cols + d] = back + turn
            turn_ref[p] = turn
        return 0

    lax.fori_loop(0, pairs_dev, weigh, 0)

    def lay(p, other, here, number):
        turn = turn_ref[p]
        turned = turn == 1
        near = rest(owner_ref[pairs_ref[0, start + p]], count)
        far = rest(owner_ref[pairs_ref[1, start + p]], count)
        at_used = (2 * here + turn) * cols + other
        seen = used_ref[at_used]
        used_ref[at_used] = seen + 1
        slot = other * CAP + jnp.where(turned, CAP - 1 - seen, seen)
        ours = turn == here
        mine_block, their_block = (far, near) if here else (near, far)
        at = jnp.where(ours, number, SPARE)
        meta_ref[0, at] = mine_block
        meta_ref[1, at] = slot
        meta_ref[2, at] = pairs_ref[2, start + p]
        meta_ref[3, at] = other * count + their_block
        meta_ref[4, jnp.where(ours, SPARE, slot)] = mine_block
        return number + ours.astype(jnp.int32)

    number = jnp.int32(0)
    for j in range(pairs_dev):
        p = mine * pairs_dev + j
        number = lay(p, peer_ref[p], 0, number)

    def lay_asking(i, number):
        p = asking_ref[i]
        return lay(p, over(p, pairs_dev), 1, number)

    meta_ref[5, 0] = lax.fori_loop(0, asking, lay_asking, number)


def spread_columns(rows):
    turned = jnp.transpose(rows)
    return [jnp.broadcast_to(turned[:, k:k + 1], (BLOCK, LANES)) for k in range(8)]


def rounded(values):
    return values.astype(BF16).astype(F32)


def per_system(ref):
    which = lax.broadcasted_iota(jnp.int32, (LS, LANES), 0)
    out = jnp.zeros((LS, LANES), F32)
    for l in range(LS):
        out = jnp.where(which == l, ref[l], out)
    return out


def wide(column, width):
    return jnp.concatenate([column] * (width // LANES), axis=1)


def lane_fold(values):
    total = values[:, 0:LANES]
    for c in range(1, values.shape[1] // LANES):
        total = total + values[:, c * LANES:(c + 1) * LANES]
    return total


def distance(col_refs, row_vals, width):
    summed = None
    for k in range(3):
        differ = wide(col_refs[k], width) - row_vals[k]
        square = differ * differ
        summed = square if summed is None else summed + square
    summed = jnp.maximum(summed, 1e-30)
    return summed * lax.rsqrt(summed)


CREST = 4.0**0.2


def slope_of(slope_ref, l):
    return jnp.broadcast_to(slope_ref[pl.ds(l, 1), :], (CHUNK, LANES))


def kernel_value(dist, slope):
    remain = jnp.maximum(CREST - dist * wide(slope, dist.shape[1]), 0.0)
    squared = remain * remain
    return ((squared * squared) * (5.0 / CREST**4 - remain)).astype(BF16)


def sub_fold(values):
    return values[0:8, :] + values[8:16, :]


def fold_forward(forward_ref, s):
    lane = lax.broadcasted_iota(jnp.int32, (LANES, LANES), 1)
    out = []
    for part in range(BLOCK // LANES):
        held = jnp.zeros((LANES, LANES), F32)
        for l in range(LS):
            block = forward_ref[s, l, part * LANES:(part + 1) * LANES, :]
            held = jnp.where(lane == l, jnp.sum(block, axis=1, keepdims=True), held)
        out.append(jnp.transpose(held)[0:LS, :])
    return jnp.concatenate(out, axis=1)


def partner_rows(far_ref, which):
    both = far_ref[over(which, 2)]
    return jnp.where(rest(which, 2) == 1, both[4:8, :], both[0:4, :])


def own_tiles(common, s, ls_ref, loc_ref, vec_ref, coord_ref, col_ref, dist_ref, forward_ref, out_ref):
    parts = BLOCK // LANES
    per = LANES // CHUNK
    turns = LS // 2
    for part in range(parts):
        low = part * LANES
        width = BLOCK - low
        rows = [loc_ref[s, k:k + 1, low:] for k in range(3)]

        def measure(c, _):
            at = pl.ds(pl.multiple_of(low + c * CHUNK, CHUNK), CHUNK)
            dist_ref[at, low:] = distance([coord_ref[k, at, :] for k in range(3)], rows, width)
            return 0

        lax.fori_loop(0, per, measure, 0, unroll=8)

    def two(t, _):
        back = [jnp.zeros((8, BLOCK), F32) for _ in range(2)]
        ids = [2 * t, 2 * t + 1]
        slopes = [slope_of(ls_ref, l) for l in ids]
        for part in range(parts):
            low = part * LANES
            width = BLOCK - low
            if common:
                rows = [rounded(loc_ref[s, 3:4, low:])] * 2
            else:
                rows = [vec_ref[s, pl.ds(l, 1), :][:, low:] for l in ids]

            def step(c, held):
                at = slice(low + c * CHUNK, low + (c + 1) * CHUNK)
                dist = dist_ref[at, low:]
                fresh = []
                for n in range(2):
                    value = kernel_value(dist, slopes[n]).astype(F32)
                    forward_ref[ids[n], at, :] = lane_fold(value * rows[n])
                    if width > LANES:
                        column = coord_ref[3, at, :] if common else col_ref[ids[n], at, :]
                        right = value[:, LANES:] * wide(column, width - LANES)
                        fresh.append(held[n] + sub_fold(right))
                return tuple(fresh) if fresh else held

            start = max(width - LANES, LANES)
            held = tuple(jnp.zeros((8, start), F32) for _ in range(2))
            for c in range(per):
                held = step(c, held)
            if width > LANES:
                for n in range(2):
                    back[n] = jnp.concatenate(
                        [back[n][:, :low + LANES], back[n][:, low + LANES:] + held[n]], axis=1
                    )
        for n in range(2):
            out_ref[pl.ds(ids[n], 1), :] = jnp.sum(back[n], axis=0, keepdims=True)
        return 0

    lax.fori_loop(0, turns, two, 0)


def own_kernel(common, ls_ref, loc_ref, vec_ref, out_ref, coord_ref, col_ref, dist_ref, forward_ref):
    def block(s, _):
        columns = spread_columns(loc_ref[s])
        for k in range(4):
            coord_ref[k] = columns[k]
        if common:
            coord_ref[3] = rounded(columns[3])
        else:
            columns = spread_columns(vec_ref[s])
            for l in range(LS):
                col_ref[l] = columns[l]
        own_tiles(
            common, s, ls_ref, loc_ref, vec_ref, coord_ref, col_ref, dist_ref, forward_ref.at[0], out_ref.at[s]
        )
        out_ref[s] = out_ref[s] + fold_forward(forward_ref, 0)
        return 0

    lax.fori_loop(0, APART, block, 0)


def first_kernel(
    ls_ref, meta_ref, loc_ref, far_hbm_ref,
    out_ref, back_ref, tiles_ref,
    coord_ref, dist_ref, forward_ref, stage_ref, far_ref, sem_ref, far_sem,
):
    count = loc_ref.shape[0]
    pair_count = meta_ref[5, 0]
    steps = BLOCK // CHUNK
    (far_copy,) = start_copies((far_hbm_ref,), (far_ref,), far_sem)
    for s in range(count):
        columns = spread_columns(loc_ref[s])
        for k in range(3):
            coord_ref[s, k] = columns[k]
        coord_ref[s, 3] = rounded(columns[3])
    for s in range(APART):
        forward_ref[s] = jnp.zeros(forward_ref.shape[1:], F32)
        out_ref[s] = jnp.zeros(out_ref.shape[1:], F32)

    def own(s, _):
        own_tiles(
            True, s, ls_ref, loc_ref, None, coord_ref.at[s], None, dist_ref, forward_ref.at[s], out_ref.at[s]
        )
        return 0

    lax.fori_loop(APART, count, own, 0)
    far_copy.wait()

    def store_copy(slot, number):
        return pltpu.make_async_copy(stage_ref.at[slot], tiles_ref.at[number], sem_ref.at[slot])

    def pair(p, number):
        a = meta_ref[0, p]
        q = meta_ref[1, p]
        reach = meta_ref[2, p]
        mine = partner_rows(far_ref, meta_ref[3, p])
        rows = [mine[k:k + 1, :] for k in range(3)]
        values = rounded(mine[3:4, :])

        def measure(c, _):
            at = pl.ds(pl.multiple_of(c * CHUNK, CHUNK), CHUNK)
            dist_ref[at, :] = distance([coord_ref[a, k, at, :] for k in range(3)], rows, BLOCK)
            return 0

        lax.fori_loop(0, steps, measure, 0, unroll=32)
        back_ref[q] = jnp.zeros((LS, BLOCK), F32)

        def sweep(ids, number):
            slopes = [slope_of(ls_ref, l) for l in ids]
            slots = [(number + n) % 4 for n in range(len(ids))]
            for n in range(len(ids)):
                @pl.when(number + n >= 4)
                def _():
                    store_copy(slots[n], number + n).wait()

            def step(c, held):
                at = pl.ds(pl.multiple_of(c * CHUNK, CHUNK), CHUNK)
                dist = dist_ref[at, :]
                column = wide(coord_ref[a, 3, at, :], BLOCK)
                fresh = []
                for n in range(len(ids)):
                    value = kernel_value(dist, slopes[n])
                    stage_ref[slots[n], at, :] = value
                    value = value.astype(F32)
                    forward_ref[a, ids[n], at, :] += lane_fold(value * values)
                    fresh.append(held[n] + sub_fold(value * column))
                return tuple(fresh)

            held = tuple(jnp.zeros((8, BLOCK), F32) for _ in ids)
            held = lax.fori_loop(0, steps, step, held, unroll=16)
            for n in range(len(ids)):
                back_ref[q, pl.ds(ids[n], 1), :] = jnp.sum(held[n], axis=0, keepdims=True)
                store_copy(slots[n], number + n).start()
            return number + len(ids)

        live = LS - reach

        def two(t, number):
            return sweep([LS - 1 - 2 * t, LS - 2 - 2 * t], number)

        number = lax.fori_loop(0, live // 2, two, number)
        return lax.cond(live % 2 == 1, lambda m: sweep([reach], m), lambda m: m, number)

    number = lax.fori_loop(0, pair_count, pair, jnp.int32(0))
    for back in range(4):
        @pl.when(number > back)
        def _():
            store_copy((number - 1 - back) % 4, number - 1 - back).wait()

    for s in range(count):
        out_ref[s] = out_ref[s] + fold_forward(forward_ref, s)


def combine_kernel(
    meta_ref, loc_ref, own_ref, fwd_ref, got_ref, w_ref, send_ref, dots_ref
):
    count = loc_ref.shape[0]
    slots = got_ref.shape[0]
    w_ref[...] = fwd_ref[...]
    for s in range(APART):
        w_ref[s] = w_ref[s] + own_ref[s]
    for q in range(slots):
        where = meta_ref[4, q]

        @pl.when(where >= 0)
        def _():
            w_ref[where] = w_ref[where] + got_ref[q]

    unit = 1.0 / (2.0 * BLOCK)
    products = [jnp.zeros((LS, BLOCK), F32) for _ in range(3)]
    for s in range(count):
        value = w_ref[s] * unit
        w_ref[s] = value
        target = jnp.broadcast_to(loc_ref[s, 3:4, :], (LS, BLOCK))
        products[0] = products[0] + target * target
        products[1] = products[1] + target * value
        products[2] = products[2] + value * value
    for q in range(slots):
        send_ref[q] = w_ref[jnp.maximum(meta_ref[4, q], 0)]
    lane = lax.broadcasted_iota(jnp.int32, (LS, LANES), 1)
    held = jnp.zeros((LS, LANES), F32)
    for n in range(3):
        held = jnp.where(lane == n, jnp.sum(products[n], axis=1, keepdims=True), held)
    dots_ref[...] = held


def second_kernel(
    ls_ref, meta_ref, loc_ref, w_ref, own_ref, dots_ref, far_pts_hbm_ref, far_hbm_ref, tiles_ref,
    out_ref, back_ref,
    list_ref, coord_ref, col_ref, dist_ref, forward_ref, wz_ref, yz_ref, stage_ref, far_pts_ref, far_ref,
    sem_ref, far_sem,
):
    count = w_ref.shape[0]
    pair_count = meta_ref[5, 0]
    steps = BLOCK // CHUNK
    depth = stage_ref.shape[0]
    copies = start_copies((far_pts_hbm_ref, far_hbm_ref), (far_pts_ref, far_ref), far_sem)

    def list_pair(p, number):
        reach = meta_ref[2, p]
        live = LS - reach

        def two(t, number):
            list_ref[number] = p * LS + LS - 1 - t
            return number + 1

        return lax.fori_loop(0, live, two, number)

    number = lax.fori_loop(0, pair_count, list_pair, jnp.int32(0))

    def load_copy(t):
        slot = t % depth
        return pltpu.make_async_copy(tiles_ref.at[t], stage_ref.at[slot], sem_ref.at[slot])

    for t in range(depth - 1):
        @pl.when(t < number)
        def _():
            load_copy(jnp.int32(t)).start()


    def clear(p, _):
        q = meta_ref[1, p]
        back_ref[over(q, CAP), pl.ds(pl.multiple_of(rest(q, CAP) * LS, LS), LS), :BLOCK] = jnp.zeros((LS, BLOCK), F32)
        return 0

    lax.fori_loop(0, pair_count, clear, 0)
    for s in range(count):
        columns = spread_columns(w_ref[s])
        for l in range(LS):
            col_ref[s, l] = columns[l]
    for s in range(APART):
        forward_ref[s] = jnp.zeros(forward_ref.shape[1:], F32)
        out_ref[s] = own_ref[s]

    def own(s, _):
        columns = spread_columns(loc_ref[s])
        for k in range(3):
            coord_ref[k] = columns[k]
        own_tiles(
            False, s, ls_ref, loc_ref, w_ref, coord_ref, col_ref.at[s], dist_ref, forward_ref.at[s], out_ref.at[s]
        )
        return 0

    lax.fori_loop(APART, count, own, 0)
    for copy in copies:
        copy.wait()
    wz_ref[...] = jnp.zeros(wz_ref.shape, F32)
    yz_ref[...] = jnp.zeros(yz_ref.shape, F32)

    def tile(t, _):
        entry = list_ref[t]
        p = over(entry, LS)
        l = rest(entry, LS)
        a = meta_ref[0, p]
        q = meta_ref[1, p]
        slot = t % depth

        @pl.when(t + depth - 1 < number)
        def _():
            load_copy(t + depth - 1).start()

        load_copy(t).wait()
        row = far_ref[q, pl.ds(l, 1), :]

        def step(c, held):
            at = pl.ds(pl.multiple_of(c * CHUNK, CHUNK), CHUNK)
            value = stage_ref[slot, at, :].astype(F32)
            forward_ref[a, l, at, :] += lane_fold(value * row)
            return held + sub_fold(value * wide(col_ref[a, l, at, :], BLOCK))

        held = lax.fori_loop(0, steps, step, jnp.zeros((8, BLOCK), F32), unroll=32)
        result = jnp.sum(held, axis=0, keepdims=True)
        back_ref[over(q, CAP), pl.ds(rest(q, CAP) * LS + l, 1), :BLOCK] = result
        target = partner_rows(far_pts_ref, meta_ref[3, p])[3:4, :]
        wz_ref[pl.ds(l, 1), :] += result * row
        yz_ref[pl.ds(l, 1), :] += result * target
        return 0

    lax.fori_loop(0, number, tile, 0)
    wz = wz_ref[...]
    yz = yz_ref[...]
    for s in range(count):
        value = out_ref[s] + fold_forward(forward_ref, s)
        out_ref[s] = value
        wz = wz + value * w_ref[s]
        yz = yz + value * loc_ref[s, 3:4, :]
    unit = 1.0 / (2.0 * BLOCK)
    lane = lax.broadcasted_iota(jnp.int32, (LS, LANES), 1)
    held = jnp.where(lane == 3, jnp.sum(wz, axis=1, keepdims=True) * unit, dots_ref[...])
    held = jnp.where(lane == 4, jnp.sum(yz, axis=1, keepdims=True) * unit, held)
    for c in range(back_ref.shape[0]):
        back_ref[c, 0:LS, BLOCK:] = held


SPAN = LANES // LS


def system_lanes(n):
    sub = lax.broadcasted_iota(jnp.int32, (LS, LANES), 0)
    lane = lax.broadcasted_iota(jnp.int32, (LS, LANES), 1)
    return lane == sub * SPAN + n


def dots_kernel(got_ref, dots_ref):
    held = got_ref[0, 0:LS, :]
    for c in range(1, got_ref.shape[0]):
        held = held + got_ref[c, 0:LS, :]
    row = jnp.zeros((LS, LANES), F32)
    for n in range(DOTS):
        row = jnp.where(system_lanes(n), held[:, n:n + 1], row)
    row = jnp.sum(row, axis=0, keepdims=True)
    dots_ref[...] = jnp.broadcast_to(row, dots_ref.shape)


def gather_kernel(meta_ref, part_ref, got_ref, z_ref):
    z_ref[...] = part_ref[...]
    for c in range(got_ref.shape[0]):
        for k in range(CAP):
            where = meta_ref[4, c * CAP + k]

            @pl.when(where >= 0)
            def _():
                z_ref[where] = z_ref[where] + got_ref[c, k * LS:(k + 1) * LS, :BLOCK]

    z_ref[...] = z_ref[...] * (1.0 / (2.0 * BLOCK))


def finish_kernel(noise_ref, loc_ref, w_ref, z_ref, dots_ref, sol_ref, res_ref):
    row = jnp.sum(dots_ref[...], axis=0, keepdims=True)
    spread = jnp.broadcast_to(row, (LS, LANES))
    noise = per_system(noise_ref)[:, 0:1]
    yy, yw, ww, wz, yz = [
        jnp.sum(jnp.where(system_lanes(n), spread, 0.0), axis=1, keepdims=True) for n in range(DOTS)
    ]
    curve = noise * yy + yw
    first = yy / curve
    keep = yw / curve
    fresh = first * ((yy * ww - yw * yw) / curve)
    beta = fresh / yy
    gain = keep + beta
    bend = noise * fresh * (1.0 + beta) + gain * gain * yw - gain * first * (ww + yz) + first * first * wz
    second = fresh / bend
    sol_y = first + second * gain
    sol_w = second * first
    res_y = keep - second * noise * gain
    res_w = second * (noise * first - gain) - first
    for s in range(loc_ref.shape[0]):
        target = loc_ref[s, 3:4, :]
        value = w_ref[s]
        sol_ref[:, s * BLOCK:(s + 1) * BLOCK] = sol_y * target - sol_w * value
        res_ref[:, s * BLOCK:(s + 1) * BLOCK] = res_y * target + res_w * value + sol_w * z_ref[s]


def on_device(points, targets, kd_order, lengthscales, noise_level, block_owner, block_pairs):
    cols = lax.axis_size("col")
    rows = lax.axis_size("row")
    me = (lax.axis_index("row") * cols + lax.axis_index("col")).astype(jnp.int32).reshape(1)
    total = points.shape[1]
    count = total // BLOCK
    pairs_dev = block_pairs.shape[1] // (rows * cols)
    slots = cols * CAP
    most = (cols - 1) * CAP * LS
    field = jax.ShapeDtypeStruct((count, LS, BLOCK), F32)

    loc, send, slopes = pl.pallas_call(
        order_kernel,
        out_shape=(
            jax.ShapeDtypeStruct((count, 8, BLOCK), F32),
            jax.ShapeDtypeStruct((cols * (count // 2), 8, BLOCK), F32),
            jax.ShapeDtypeStruct((LS, LANES), F32),
        ),
        in_specs=[smem_spec()] + [hbm_spec()] * 3,
        out_specs=(vmem_spec(),) * 3,
        scratch_shapes=[
            VMEM((3, total), F32),
            VMEM((1, total), F32),
            VMEM((1, total), jnp.int32),
            pltpu.SemaphoreType.DMA((3,)),
        ],
        compiler_params=params(8),
        name="order",
    )(lengthscales, points, targets.reshape(1, total), kd_order.reshape(1, total))
    def own(vec, common):
        return pl.pallas_call(
            lambda *refs: own_kernel(common, *refs),
            out_shape=jax.ShapeDtypeStruct((APART, LS, BLOCK), F32),
            in_specs=[vmem_spec(), vmem_spec(), vmem_spec()],
            out_specs=vmem_spec(),
            scratch_shapes=[
                VMEM((4, BLOCK, LANES), F32),
                VMEM((LS, BLOCK, LANES), F32),
                VMEM((BLOCK, BLOCK), F32),
                VMEM((1, LS, BLOCK, LANES), F32),
            ],
            compiler_params=params(16),
            cost_estimate=pl.CostEstimate(flops=2 * 10**9, bytes_accessed=10**6, transcendentals=0),
            name="own_first" if common else "own_second",
        )(slopes, loc, vec)

    far = lax.all_to_all(send, "col", split_axis=0, concat_axis=0, tiled=True)
    meta = pl.pallas_call(
        lambda *refs: plan_kernel(cols, count, pairs_dev, *refs),
        out_shape=jax.ShapeDtypeStruct((8, SPARE + 1), jnp.int32),
        in_specs=[smem_spec(), hbm_spec(), hbm_spec()],
        out_specs=smem_spec(),
        scratch_shapes=[
            SMEM((n,), jnp.int32)
            for n in [cols * pairs_dev] * 3 + [cols, cols * cols, cols * pairs_dev + 1, 4 * cols]
        ] + [
            SMEM(block_owner.shape, jnp.int32),
            SMEM(block_pairs.shape, jnp.int32),
            pltpu.SemaphoreType.DMA((2,)),
        ],
        compiler_params=params(8),
        cost_estimate=pl.CostEstimate(flops=10**9, bytes_accessed=10**6, transcendentals=0),
        name="plan",
    )(me, block_owner, block_pairs)
    own_one = own(loc, True)
    fwd_one, back_one, tiles = pl.pallas_call(
        first_kernel,
        out_shape=(
            field,
            jax.ShapeDtypeStruct((slots, LS, BLOCK), F32),
            jax.ShapeDtypeStruct((most, BLOCK, BLOCK), BF16),
        ),
        in_specs=[vmem_spec(), smem_spec(), vmem_spec(), any_spec()],
        out_specs=(vmem_spec(), vmem_spec(), any_spec()),
        scratch_shapes=[
            VMEM((count, 4, BLOCK, LANES), F32),
            VMEM((BLOCK, BLOCK), F32),
            VMEM((count, LS, BLOCK, LANES), F32),
            VMEM((4, BLOCK, BLOCK), BF16),
            VMEM((slots, LS, BLOCK), F32),
            pltpu.SemaphoreType.DMA((4,)),
            pltpu.SemaphoreType.DMA((1,)),
        ],
        compiler_params=params(28),
        cost_estimate=pl.CostEstimate(flops=10**10, bytes_accessed=6 * 10**7, transcendentals=0),
        name="cross_first",
    )(slopes, meta, loc, far)
    got_one = lax.all_to_all(back_one, "col", split_axis=0, concat_axis=0, tiled=True)

    w, send_w, dots_one = pl.pallas_call(
        combine_kernel,
        out_shape=(
            field,
            jax.ShapeDtypeStruct((slots, LS, BLOCK), F32),
            jax.ShapeDtypeStruct((LS, LANES), F32),
        ),
        in_specs=[smem_spec()] + [vmem_spec()] * 4,
        out_specs=(vmem_spec(),) * 3,
        compiler_params=params(8),
        name="combine",
    )(meta, loc, own_one, fwd_one, got_one)
    far_w = lax.all_to_all(send_w, "col", split_axis=0, concat_axis=0, tiled=True)
    own_two = own(w, False)
    fwd_two, back_two = pl.pallas_call(
        second_kernel,
        out_shape=(field, jax.ShapeDtypeStruct((cols, CAP * LS, BLOCK + LANES), F32)),
        in_specs=[vmem_spec(), smem_spec()] + [vmem_spec()] * 4 + [any_spec()] * 3,
        out_specs=(vmem_spec(),) * 2,
        scratch_shapes=[
            SMEM((most,), jnp.int32),
            VMEM((3, BLOCK, LANES), F32),
            VMEM((count, LS, BLOCK, LANES), F32),
            VMEM((BLOCK, BLOCK), F32),
            VMEM((count, LS, BLOCK, LANES), F32),
            VMEM((LS, BLOCK), F32),
            VMEM((LS, BLOCK), F32),
            VMEM((8, BLOCK, BLOCK), BF16),
            VMEM((slots, LS, BLOCK), F32),
            VMEM((slots, LS, BLOCK), F32),
            pltpu.SemaphoreType.DMA((8,)),
            pltpu.SemaphoreType.DMA((2,)),
        ],
        compiler_params=params(40),
        cost_estimate=pl.CostEstimate(flops=5 * 10**9, bytes_accessed=6 * 10**7, transcendentals=0),
        name="cross_second",
    )(slopes, meta, loc, w, own_two, dots_one, far, far_w, tiles)
    got_two = lax.all_to_all(back_two, "col", split_axis=0, concat_axis=0, tiled=True)

    dots_two = pl.pallas_call(
        dots_kernel,
        out_shape=jax.ShapeDtypeStruct((rows, LANES), F32),
        in_specs=[pl.BlockSpec((cols, LS, LANES), lambda i: (0, 0, BLOCK // LANES))],
        out_specs=pl.BlockSpec((rows, LANES), lambda i: (0, 0)),
        grid=(1,),
        compiler_params=params(4),
        name="dots",
    )(got_two)
    dots = lax.all_to_all(dots_two, "row", split_axis=0, concat_axis=0, tiled=True)
    z = pl.pallas_call(
        gather_kernel,
        out_shape=field,
        in_specs=[smem_spec()] + [vmem_spec()] * 2,
        out_specs=vmem_spec(),
        compiler_params=params(8),
        cost_estimate=pl.CostEstimate(flops=10**8, bytes_accessed=2 * 10**6, transcendentals=0),
        name="gather",
    )(meta, fwd_two, got_two)
    return pl.pallas_call(
        finish_kernel,
        out_shape=(jax.ShapeDtypeStruct((LS, total), F32),) * 2,
        in_specs=[smem_spec()] + [vmem_spec()] * 4,
        out_specs=(vmem_spec(),) * 2,
        compiler_params=params(8),
        name="finish",
    )(noise_level, loc, w, z, dots)


def solution(mesh):
    placed = (P(None, ("row", "col")), P(("row", "col")), P(("row", "col")), P(), P(), P(), P())
    return jax.shard_map(
        on_device,
        mesh=mesh,
        in_specs=placed,
        out_specs=(P(None, ("row", "col")), P(None, ("row", "col"))),
        check_vma=False,
    )
```

```python
import jax
import jax.numpy as jnp
from jax import lax
from jax.experimental import pallas as pl
from jax.experimental.pallas import tpu as pltpu
from jax.sharding import PartitionSpec as P

BLOCK = 512
LS = 8
CAP = 2
LANES = 128
CHUNK = 16
DOTS = 5
APART = 2
F32 = jnp.float32
BF16 = jnp.bfloat16
VMEM = pltpu.VMEM
SMEM = pltpu.SMEM


def vmem_spec():
    return pl.BlockSpec(memory_space=pltpu.VMEM)


def smem_spec():
    return pl.BlockSpec(memory_space=pltpu.SMEM)


def any_spec():
    return pl.BlockSpec(memory_space=pl.ANY)


def hbm_spec():
    return pl.BlockSpec(memory_space=pltpu.HBM)


def start_copies(sources, targets, sems):
    copies = [pltpu.make_async_copy(a, b, sems.at[n]) for n, (a, b) in enumerate(zip(sources, targets))]
    for copy in copies:
        copy.start()
    return copies


def params(mebibytes):
    return pltpu.CompilerParams(vmem_limit_bytes=mebibytes * 2**20)


def over(value, size):
    return value >> (size.bit_length() - 1) if size & (size - 1) == 0 else value // size


def rest(value, size):
    return value & (size - 1) if size & (size - 1) == 0 else value % size


def order_kernel(scale_ref, pts_hbm, tgt_hbm, order_hbm, loc_ref, send_ref, slope_ref, pts_ref, tgt_ref, order_ref, sems):
    for copy in start_copies((pts_hbm, tgt_hbm, order_hbm), (pts_ref, tgt_ref, order_ref), sems):
        copy.wait()
    slope_ref[...] = CREST / per_system(scale_ref)
    total = pts_ref.shape[1]
    pieces = total // LANES
    per = BLOCK // LANES
    source = jnp.concatenate([pts_ref[...], tgt_ref[...], jnp.zeros((4, total), F32)], axis=0)
    for o in range(pieces):
        index = jnp.broadcast_to(order_ref[:, o * LANES:(o + 1) * LANES], (8, LANES))
        high = over(index, LANES)
        low = rest(index, LANES)
        got = jnp.zeros((8, LANES), F32)
        for c in range(pieces):
            part = jnp.take_along_axis(
                source[:, c * LANES:(c + 1) * LANES], low, axis=1, mode="promise_in_bounds"
            )
            got = jnp.where(high == c, part, got)
        loc_ref[o // per, :, (o % per) * LANES:(o % per + 1) * LANES] = got
    halves = []
    for h in range(loc_ref.shape[0] // 2):
        halves.append(jnp.concatenate([loc_ref[2 * h, 0:4, :], loc_ref[2 * h + 1, 0:4, :]], axis=0))
    for c in range(send_ref.shape[0] // len(halves)):
        for h in range(len(halves)):
            send_ref[c * len(halves) + h] = halves[h]


SPARE = 63


def plan_kernel(cols, count, pairs_dev, me_ref, owner_hbm, pairs_hbm, meta_ref, peer_ref, cost_ref, turn_ref, load_ref, have_ref, asking_ref, used_ref, owner_ref, pairs_ref, sems):
    copies = start_copies((owner_hbm, pairs_hbm), (owner_ref, pairs_ref), sems)
    mine = rest(me_ref[0], cols)
    start = over(me_ref[0], cols) * (cols * pairs_dev)

    def clear(i, _):
        for c in range(cols):
            have_ref[i * cols + c] = 0
        for c in range(4):
            used_ref[c * cols + i] = 0
        return 0

    lax.fori_loop(0, cols, clear, 0)
    for q in range(cols * CAP):
        meta_ref[4, q] = -1
    for copy in copies:
        copy.wait()

    def read(d, asking):
        total = jnp.int32(0)
        for j in range(pairs_dev):
            p = d * pairs_dev + j
            e = rest(over(owner_ref[pairs_ref[1, start + p]], count), cols)
            cost = 4 * (LS - pairs_ref[2, start + p]) + 3
            peer_ref[p] = e
            cost_ref[p] = cost
            total = total + cost
            have_ref[d * cols + e] = have_ref[d * cols + e] + 1
            asking_ref[asking] = p
            asking = asking + (e == mine).astype(jnp.int32)
        load_ref[d] = total
        return asking

    asking = lax.fori_loop(0, cols, read, jnp.int32(0))

    def weigh(j, _):
        for d in range(cols):
            p = d * pairs_dev + j
            e = peer_ref[p]
            cost = cost_ref[p]
            here = load_ref[d]
            there = load_ref[e]
            back = have_ref[e * cols + d]
            turn = jnp.logical_and(here - there > cost, back < CAP).astype(jnp.int32)
            load_ref[d] = here - turn * cost
            load_ref[e] = there + turn * cost
            have_ref[e * cols + d] = back + turn
            turn_ref[p] = turn
        return 0

    lax.fori_loop(0, pairs_dev, weigh, 0)

    def lay(p, other, here, number):
        turn = turn_ref[p]
        turned = turn == 1
        near = rest(owner_ref[pairs_ref[0, start + p]], count)
        far = rest(owner_ref[pairs_ref[1, start + p]], count)
        at_used = (2 * here + turn) * cols + other
        seen = used_ref[at_used]
        used_ref[at_used] = seen + 1
        slot = other * CAP + jnp.where(turned, CAP - 1 - seen, seen)
        ours = turn == here
        mine_block, their_block = (far, near) if here else (near, far)
        at = jnp.where(ours, number, SPARE)
        meta_ref[0, at] = mine_block
        meta_ref[1, at] = slot
        meta_ref[2, at] = pairs_ref[2, start + p]
        meta_ref[3, at] = other * count + their_block
        meta_ref[4, jnp.where(ours, SPARE, slot)] = mine_block
        return number + ours.astype(jnp.int32)

    number = jnp.int32(0)
    for j in range(pairs_dev):
        p = mine * pairs_dev + j
        number = lay(p, peer_ref[p], 0, number)

    def lay_asking(i, number):
        p = asking_ref[i]
        return lay(p, over(p, pairs_dev), 1, number)

    meta_ref[5, 0] = lax.fori_loop(0, asking, lay_asking, number)


def spread_columns(rows):
    turned = jnp.transpose(rows)
    return [jnp.broadcast_to(turned[:, k:k + 1], (BLOCK, LANES)) for k in range(8)]


def rounded(values):
    return values.astype(BF16).astype(F32)


def per_system(ref):
    which = lax.broadcasted_iota(jnp.int32, (LS, LANES), 0)
    out = jnp.zeros((LS, LANES), F32)
    for l in range(LS):
        out = jnp.where(which == l, ref[l], out)
    return out


def wide(column, width):
    return jnp.concatenate([column] * (width // LANES), axis=1)


def lane_fold(values):
    total = values[:, 0:LANES]
    for c in range(1, values.shape[1] // LANES):
        total = total + values[:, c * LANES:(c + 1) * LANES]
    return total


def distance(col_refs, row_vals, width):
    summed = None
    for k in range(3):
        differ = wide(col_refs[k], width) - row_vals[k]
        square = differ * differ
        summed = square if summed is None else summed + square
    summed = jnp.maximum(summed, 1e-30)
    return summed * lax.rsqrt(summed)


CREST = 4.0**0.2


def slope_of(slope_ref, l):
    return jnp.broadcast_to(slope_ref[pl.ds(l, 1), :], (CHUNK, LANES))


def kernel_value(dist, slope):
    remain = jnp.maximum(CREST - dist * wide(slope, dist.shape[1]), 0.0)
    squared = remain * remain
    return ((squared * squared) * (5.0 / CREST**4 - remain)).astype(BF16)


def sub_fold(values):
    return values[0:8, :] + values[8:16, :]


def fold_forward(forward_ref, s):
    lane = lax.broadcasted_iota(jnp.int32, (LANES, LANES), 1)
    out = []
    for part in range(BLOCK // LANES):
        held = jnp.zeros((LANES, LANES), F32)
        for l in range(LS):
            block = forward_ref[s, l, part * LANES:(part + 1) * LANES, :]
            held = jnp.where(lane == l, jnp.sum(block, axis=1, keepdims=True), held)
        out.append(jnp.transpose(held)[0:LS, :])
    return jnp.concatenate(out, axis=1)


def partner_rows(far_ref, which):
    both = far_ref[over(which, 2)]
    return jnp.where(rest(which, 2) == 1, both[4:8, :], both[0:4, :])


def own_tiles(common, s, ls_ref, loc_ref, vec_ref, coord_ref, col_ref, dist_ref, forward_ref, out_ref):
    parts = BLOCK // LANES
    per = LANES // CHUNK
    turns = LS // 2
    for part in range(parts):
        low = part * LANES
        width = BLOCK - low
        rows = [loc_ref[s, k:k + 1, low:] for k in range(3)]

        def measure(c, _):
            at = pl.ds(pl.multiple_of(low + c * CHUNK, CHUNK), CHUNK)
            dist_ref[at, low:] = distance([coord_ref[k, at, :] for k in range(3)], rows, width)
            return 0

        lax.fori_loop(0, per, measure, 0, unroll=8)

    def two(t, _):
        back = [jnp.zeros((8, BLOCK), F32) for _ in range(2)]
        ids = [2 * t, 2 * t + 1]
        slopes = [slope_of(ls_ref, l) for l in ids]
        for part in range(parts):
            low = part * LANES
            width = BLOCK - low
            if common:
                rows = [rounded(loc_ref[s, 3:4, low:])] * 2
            else:
                rows = [vec_ref[s, pl.ds(l, 1), :][:, low:] for l in ids]

            def step(c, held):
                at = slice(low + c * CHUNK, low + (c + 1) * CHUNK)
                dist = dist_ref[at, low:]
                fresh = []
                for n in range(2):
                    value = kernel_value(dist, slopes[n]).astype(F32)
                    forward_ref[ids[n], at, :] = lane_fold(value * rows[n])
                    if width > LANES:
                        column = coord_ref[3, at, :] if common else col_ref[ids[n], at, :]
                        right = value[:, LANES:] * wide(column, width - LANES)
                        fresh.append(held[n] + sub_fold(right))
                return tuple(fresh) if fresh else held

            start = max(width - LANES, LANES)
            held = tuple(jnp.zeros((8, start), F32) for _ in range(2))
            for c in range(per):
                held = step(c, held)
            if width > LANES:
                for n in range(2):
                    back[n] = jnp.concatenate(
                        [back[n][:, :low + LANES], back[n][:, low + LANES:] + held[n]], axis=1
                    )
        for n in range(2):
            out_ref[pl.ds(ids[n], 1), :] = jnp.sum(back[n], axis=0, keepdims=True)
        return 0

    lax.fori_loop(0, turns, two, 0)


def own_kernel(common, ls_ref, loc_ref, vec_ref, out_ref, coord_ref, col_ref, dist_ref, forward_ref):
    def block(s, _):
        columns = spread_columns(loc_ref[s])
        for k in range(4):
            coord_ref[k] = columns[k]
        if common:
            coord_ref[3] = rounded(columns[3])
        else:
            columns = spread_columns(vec_ref[s])
            for l in range(LS):
                col_ref[l] = columns[l]
        own_tiles(
            common, s, ls_ref, loc_ref, vec_ref, coord_ref, col_ref, dist_ref, forward_ref.at[0], out_ref.at[s]
        )
        out_ref[s] = out_ref[s] + fold_forward(forward_ref, 0)
        return 0

    lax.fori_loop(0, APART, block, 0)


def first_kernel(
    ls_ref, meta_ref, loc_ref, far_hbm_ref,
    out_ref, back_ref, tiles_ref,
    coord_ref, dist_ref, forward_ref, stage_ref, far_ref, sem_ref, far_sem,
):
    count = loc_ref.shape[0]
    pair_count = meta_ref[5, 0]
    steps = BLOCK // CHUNK
    (far_copy,) = start_copies((far_hbm_ref,), (far_ref,), far_sem)
    for s in range(count):
        columns = spread_columns(loc_ref[s])
        for k in range(3):
            coord_ref[s, k] = columns[k]
        coord_ref[s, 3] = rounded(columns[3])
    for s in range(APART):
        forward_ref[s] = jnp.zeros(forward_ref.shape[1:], F32)
        out_ref[s] = jnp.zeros(out_ref.shape[1:], F32)

    def own(s, _):
        own_tiles(
            True, s, ls_ref, loc_ref, None, coord_ref.at[s], None, dist_ref, forward_ref.at[s], out_ref.at[s]
        )
        return 0

    lax.fori_loop(APART, count, own, 0)
    far_copy.wait()

    def store_copy(slot, number):
        return pltpu.make_async_copy(stage_ref.at[slot], tiles_ref.at[number], sem_ref.at[slot])

    def pair(p, number):
        a = meta_ref[0, p]
        q = meta_ref[1, p]
        reach = meta_ref[2, p]
        mine = partner_rows(far_ref, meta_ref[3, p])
        rows = [mine[k:k + 1, :] for k in range(3)]
        values = rounded(mine[3:4, :])

        def measure(c, _):
            at = pl.ds(pl.multiple_of(c * CHUNK, CHUNK), CHUNK)
            dist_ref[at, :] = distance([coord_ref[a, k, at, :] for k in range(3)], rows, BLOCK)
            return 0

        lax.fori_loop(0, steps, measure, 0, unroll=32)
        back_ref[q] = jnp.zeros((LS, BLOCK), F32)

        def sweep(ids, number):
            slopes = [slope_of(ls_ref, l) for l in ids]
            slots = [(number + n) % 4 for n in range(len(ids))]
            for n in range(len(ids)):
                @pl.when(number + n >= 4)
                def _():
                    store_copy(slots[n], number + n).wait()

            def step(c, held):
                at = pl.ds(pl.multiple_of(c * CHUNK, CHUNK), CHUNK)
                dist = dist_ref[at, :]
                column = wide(coord_ref[a, 3, at, :], BLOCK)
                fresh = []
                for n in range(len(ids)):
                    value = kernel_value(dist, slopes[n])
                    stage_ref[slots[n], at, :] = value
                    value = value.astype(F32)
                    forward_ref[a, ids[n], at, :] += lane_fold(value * values)
                    fresh.append(held[n] + sub_fold(value * column))
                return tuple(fresh)

            held = tuple(jnp.zeros((8, BLOCK), F32) for _ in ids)
            held = lax.fori_loop(0, steps, step, held, unroll=32)
            for n in range(len(ids)):
                back_ref[q, pl.ds(ids[n], 1), :] = jnp.sum(held[n], axis=0, keepdims=True)
                store_copy(slots[n], number + n).start()
            return number + len(ids)

        live = LS - reach

        def two(t, number):
            return sweep([LS - 1 - 2 * t, LS - 2 - 2 * t], number)

        number = lax.fori_loop(0, live // 2, two, number)
        return lax.cond(live % 2 == 1, lambda m: sweep([reach], m), lambda m: m, number)

    number = lax.fori_loop(0, pair_count, pair, jnp.int32(0))
    for back in range(4):
        @pl.when(number > back)
        def _():
            store_copy((number - 1 - back) % 4, number - 1 - back).wait()

    for s in range(count):
        out_ref[s] = out_ref[s] + fold_forward(forward_ref, s)


def combine_kernel(
    meta_ref, loc_ref, own_ref, fwd_ref, got_ref, w_ref, send_ref, dots_ref
):
    count = loc_ref.shape[0]
    slots = got_ref.shape[0]
    w_ref[...] = fwd_ref[...]
    for s in range(APART):
        w_ref[s] = w_ref[s] + own_ref[s]
    for q in range(slots):
        where = meta_ref[4, q]

        @pl.when(where >= 0)
        def _():
            w_ref[where] = w_ref[where] + got_ref[q]

    unit = 1.0 / (2.0 * BLOCK)
    products = [jnp.zeros((LS, BLOCK), F32) for _ in range(3)]
    for s in range(count):
        value = w_ref[s] * unit
        w_ref[s] = value
        target = jnp.broadcast_to(loc_ref[s, 3:4, :], (LS, BLOCK))
        products[0] = products[0] + target * target
        products[1] = products[1] + target * value
        products[2] = products[2] + value * value
    for q in range(slots):
        send_ref[q] = w_ref[jnp.maximum(meta_ref[4, q], 0)]
    lane = lax.broadcasted_iota(jnp.int32, (LS, LANES), 1)
    held = jnp.zeros((LS, LANES), F32)
    for n in range(3):
        held = jnp.where(lane == n, jnp.sum(products[n], axis=1, keepdims=True), held)
    dots_ref[...] = held


def second_kernel(
    ls_ref, meta_ref, loc_ref, w_ref, own_ref, dots_ref, far_pts_hbm_ref, far_hbm_ref, tiles_ref,
    out_ref, back_ref,
    list_ref, coord_ref, col_ref, dist_ref, forward_ref, wz_ref, yz_ref, stage_ref, far_pts_ref, far_ref,
    sem_ref, far_sem,
):
    count = w_ref.shape[0]
    pair_count = meta_ref[5, 0]
    steps = BLOCK // CHUNK
    depth = stage_ref.shape[0]
    copies = start_copies((far_pts_hbm_ref, far_hbm_ref), (far_pts_ref, far_ref), far_sem)

    def list_pair(p, number):
        reach = meta_ref[2, p]
        live = LS - reach

        def two(t, number):
            list_ref[number] = p * LS + LS - 1 - t
            return number + 1

        return lax.fori_loop(0, live, two, number)

    number = lax.fori_loop(0, pair_count, list_pair, jnp.int32(0))

    def load_copy(t):
        slot = t % depth
        return pltpu.make_async_copy(tiles_ref.at[t], stage_ref.at[slot], sem_ref.at[slot])

    for t in range(depth - 1):
        @pl.when(t < number)
        def _():
            load_copy(jnp.int32(t)).start()


    def clear(p, _):
        q = meta_ref[1, p]
        back_ref[over(q, CAP), pl.ds(pl.multiple_of(rest(q, CAP) * LS, LS), LS), :BLOCK] = jnp.zeros((LS, BLOCK), F32)
        return 0

    lax.fori_loop(0, pair_count, clear, 0)
    for s in range(count):
        columns = spread_columns(w_ref[s])
        for l in range(LS):
            col_ref[s, l] = columns[l]
    for s in range(APART):
        forward_ref[s] = jnp.zeros(forward_ref.shape[1:], F32)
        out_ref[s] = own_ref[s]

    def own(s, _):
        columns = spread_columns(loc_ref[s])
        for k in range(3):
            coord_ref[k] = columns[k]
        own_tiles(
            False, s, ls_ref, loc_ref, w_ref, coord_ref, col_ref.at[s], dist_ref, forward_ref.at[s], out_ref.at[s]
        )
        return 0

    lax.fori_loop(APART, count, own, 0)
    for copy in copies:
        copy.wait()
    wz_ref[...] = jnp.zeros(wz_ref.shape, F32)
    yz_ref[...] = jnp.zeros(yz_ref.shape, F32)

    def tile(t, _):
        entry = list_ref[t]
        p = over(entry, LS)
        l = rest(entry, LS)
        a = meta_ref[0, p]
        q = meta_ref[1, p]
        slot = t % depth

        @pl.when(t + depth - 1 < number)
        def _():
            load_copy(t + depth - 1).start()

        load_copy(t).wait()
        row = far_ref[q, pl.ds(l, 1), :]

        def step(c, held):
            at = pl.ds(pl.multiple_of(c * CHUNK, CHUNK), CHUNK)
            value = stage_ref[slot, at, :].astype(F32)
            forward_ref[a, l, at, :] += lane_fold(value * row)
            return held + sub_fold(value * wide(col_ref[a, l, at, :], BLOCK))

        held = lax.fori_loop(0, steps, step, jnp.zeros((8, BLOCK), F32), unroll=32)
        result = jnp.sum(held, axis=0, keepdims=True)
        back_ref[over(q, CAP), pl.ds(rest(q, CAP) * LS + l, 1), :BLOCK] = result
        target = partner_rows(far_pts_ref, meta_ref[3, p])[3:4, :]
        wz_ref[pl.ds(l, 1), :] += result * row
        yz_ref[pl.ds(l, 1), :] += result * target
        return 0

    lax.fori_loop(0, number, tile, 0)
    wz = wz_ref[...]
    yz = yz_ref[...]
    for s in range(count):
        value = out_ref[s] + fold_forward(forward_ref, s)
        out_ref[s] = value
        wz = wz + value * w_ref[s]
        yz = yz + value * loc_ref[s, 3:4, :]
    unit = 1.0 / (2.0 * BLOCK)
    lane = lax.broadcasted_iota(jnp.int32, (LS, LANES), 1)
    held = jnp.where(lane == 3, jnp.sum(wz, axis=1, keepdims=True) * unit, dots_ref[...])
    held = jnp.where(lane == 4, jnp.sum(yz, axis=1, keepdims=True) * unit, held)
    for c in range(back_ref.shape[0]):
        back_ref[c, 0:LS, BLOCK:] = held


SPAN = LANES // LS


def system_lanes(n):
    sub = lax.broadcasted_iota(jnp.int32, (LS, LANES), 0)
    lane = lax.broadcasted_iota(jnp.int32, (LS, LANES), 1)
    return lane == sub * SPAN + n


def dots_kernel(got_ref, dots_ref):
    held = got_ref[0, 0:LS, :]
    for c in range(1, got_ref.shape[0]):
        held = held + got_ref[c, 0:LS, :]
    row = jnp.zeros((LS, LANES), F32)
    for n in range(DOTS):
        row = jnp.where(system_lanes(n), held[:, n:n + 1], row)
    row = jnp.sum(row, axis=0, keepdims=True)
    dots_ref[...] = jnp.broadcast_to(row, dots_ref.shape)


def gather_kernel(meta_ref, part_ref, got_ref, z_ref):
    z_ref[...] = part_ref[...]
    for c in range(got_ref.shape[0]):
        for k in range(CAP):
            where = meta_ref[4, c * CAP + k]

            @pl.when(where >= 0)
            def _():
                z_ref[where] = z_ref[where] + got_ref[c, k * LS:(k + 1) * LS, :BLOCK]

    z_ref[...] = z_ref[...] * (1.0 / (2.0 * BLOCK))


def finish_kernel(noise_ref, loc_ref, w_ref, z_ref, dots_ref, sol_ref, res_ref):
    row = jnp.sum(dots_ref[...], axis=0, keepdims=True)
    spread = jnp.broadcast_to(row, (LS, LANES))
    noise = per_system(noise_ref)[:, 0:1]
    yy, yw, ww, wz, yz = [
        jnp.sum(jnp.where(system_lanes(n), spread, 0.0), axis=1, keepdims=True) for n in range(DOTS)
    ]
    curve = noise * yy + yw
    first = yy / curve
    keep = yw / curve
    fresh = first * ((yy * ww - yw * yw) / curve)
    beta = fresh / yy
    gain = keep + beta
    bend = noise * fresh * (1.0 + beta) + gain * gain * yw - gain * first * (ww + yz) + first * first * wz
    second = fresh / bend
    sol_y = first + second * gain
    sol_w = second * first
    res_y = keep - second * noise * gain
    res_w = second * (noise * first - gain) - first
    for s in range(loc_ref.shape[0]):
        target = loc_ref[s, 3:4, :]
        value = w_ref[s]
        sol_ref[:, s * BLOCK:(s + 1) * BLOCK] = sol_y * target - sol_w * value
        res_ref[:, s * BLOCK:(s + 1) * BLOCK] = res_y * target + res_w * value + sol_w * z_ref[s]


def on_device(points, targets, kd_order, lengthscales, noise_level, block_owner, block_pairs):
    cols = lax.axis_size("col")
    rows = lax.axis_size("row")
    me = (lax.axis_index("row") * cols + lax.axis_index("col")).astype(jnp.int32).reshape(1)
    total = points.shape[1]
    count = total // BLOCK
    pairs_dev = block_pairs.shape[1] // (rows * cols)
    slots = cols * CAP
    most = (cols - 1) * CAP * LS
    field = jax.ShapeDtypeStruct((count, LS, BLOCK), F32)

    loc, send, slopes = pl.pallas_call(
        order_kernel,
        out_shape=(
            jax.ShapeDtypeStruct((count, 8, BLOCK), F32),
            jax.ShapeDtypeStruct((cols * (count // 2), 8, BLOCK), F32),
            jax.ShapeDtypeStruct((LS, LANES), F32),
        ),
        in_specs=[smem_spec()] + [hbm_spec()] * 3,
        out_specs=(vmem_spec(),) * 3,
        scratch_shapes=[
            VMEM((3, total), F32),
            VMEM((1, total), F32),
            VMEM((1, total), jnp.int32),
            pltpu.SemaphoreType.DMA((3,)),
        ],
        compiler_params=params(8),
        name="order",
    )(lengthscales, points, targets.reshape(1, total), kd_order.reshape(1, total))
    def own(vec, common):
        return pl.pallas_call(
            lambda *refs: own_kernel(common, *refs),
            out_shape=jax.ShapeDtypeStruct((APART, LS, BLOCK), F32),
            in_specs=[vmem_spec(), vmem_spec(), vmem_spec()],
            out_specs=vmem_spec(),
            scratch_shapes=[
                VMEM((4, BLOCK, LANES), F32),
                VMEM((LS, BLOCK, LANES), F32),
                VMEM((BLOCK, BLOCK), F32),
                VMEM((1, LS, BLOCK, LANES), F32),
            ],
            compiler_params=params(16),
            cost_estimate=pl.CostEstimate(flops=2 * 10**9, bytes_accessed=10**6, transcendentals=0),
            name="own_first" if common else "own_second",
        )(slopes, loc, vec)

    far = lax.all_to_all(send, "col", split_axis=0, concat_axis=0, tiled=True)
    meta = pl.pallas_call(
        lambda *refs: plan_kernel(cols, count, pairs_dev, *refs),
        out_shape=jax.ShapeDtypeStruct((8, SPARE + 1), jnp.int32),
        in_specs=[smem_spec(), hbm_spec(), hbm_spec()],
        out_specs=smem_spec(),
        scratch_shapes=[
            SMEM((n,), jnp.int32)
            for n in [cols * pairs_dev] * 3 + [cols, cols * cols, cols * pairs_dev + 1, 4 * cols]
        ] + [
            SMEM(block_owner.shape, jnp.int32),
            SMEM(block_pairs.shape, jnp.int32),
            pltpu.SemaphoreType.DMA((2,)),
        ],
        compiler_params=params(8),
        cost_estimate=pl.CostEstimate(flops=10**9, bytes_accessed=10**6, transcendentals=0),
        name="plan",
    )(me, block_owner, block_pairs)
    own_one = own(loc, True)
    fwd_one, back_one, tiles = pl.pallas_call(
        first_kernel,
        out_shape=(
            field,
            jax.ShapeDtypeStruct((slots, LS, BLOCK), F32),
            jax.ShapeDtypeStruct((most, BLOCK, BLOCK), BF16),
        ),
        in_specs=[vmem_spec(), smem_spec(), vmem_spec(), any_spec()],
        out_specs=(vmem_spec(), vmem_spec(), any_spec()),
        scratch_shapes=[
            VMEM((count, 4, BLOCK, LANES), F32),
            VMEM((BLOCK, BLOCK), F32),
            VMEM((count, LS, BLOCK, LANES), F32),
            VMEM((4, BLOCK, BLOCK), BF16),
            VMEM((slots, LS, BLOCK), F32),
            pltpu.SemaphoreType.DMA((4,)),
            pltpu.SemaphoreType.DMA((1,)),
        ],
        compiler_params=params(28),
        cost_estimate=pl.CostEstimate(flops=10**10, bytes_accessed=6 * 10**7, transcendentals=0),
        name="cross_first",
    )(slopes, meta, loc, far)
    got_one = lax.all_to_all(back_one, "col", split_axis=0, concat_axis=0, tiled=True)

    w, send_w, dots_one = pl.pallas_call(
        combine_kernel,
        out_shape=(
            field,
            jax.ShapeDtypeStruct((slots, LS, BLOCK), F32),
            jax.ShapeDtypeStruct((LS, LANES), F32),
        ),
        in_specs=[smem_spec()] + [vmem_spec()] * 4,
        out_specs=(vmem_spec(),) * 3,
        compiler_params=params(8),
        name="combine",
    )(meta, loc, own_one, fwd_one, got_one)
    far_w = lax.all_to_all(send_w, "col", split_axis=0, concat_axis=0, tiled=True)
    own_two = own(w, False)
    fwd_two, back_two = pl.pallas_call(
        second_kernel,
        out_shape=(field, jax.ShapeDtypeStruct((cols, CAP * LS, BLOCK + LANES), F32)),
        in_specs=[vmem_spec(), smem_spec()] + [vmem_spec()] * 4 + [any_spec()] * 3,
        out_specs=(vmem_spec(),) * 2,
        scratch_shapes=[
            SMEM((most,), jnp.int32),
            VMEM((3, BLOCK, LANES), F32),
            VMEM((count, LS, BLOCK, LANES), F32),
            VMEM((BLOCK, BLOCK), F32),
            VMEM((count, LS, BLOCK, LANES), F32),
            VMEM((LS, BLOCK), F32),
            VMEM((LS, BLOCK), F32),
            VMEM((8, BLOCK, BLOCK), BF16),
            VMEM((slots, LS, BLOCK), F32),
            VMEM((slots, LS, BLOCK), F32),
            pltpu.SemaphoreType.DMA((8,)),
            pltpu.SemaphoreType.DMA((2,)),
        ],
        compiler_params=params(40),
        cost_estimate=pl.CostEstimate(flops=5 * 10**9, bytes_accessed=6 * 10**7, transcendentals=0),
        name="cross_second",
    )(slopes, meta, loc, w, own_two, dots_one, far, far_w, tiles)
    got_two = lax.all_to_all(back_two, "col", split_axis=0, concat_axis=0, tiled=True)

    dots_two = pl.pallas_call(
        dots_kernel,
        out_shape=jax.ShapeDtypeStruct((rows, LANES), F32),
        in_specs=[pl.BlockSpec((cols, LS, LANES), lambda i: (0, 0, BLOCK // LANES))],
        out_specs=pl.BlockSpec((rows, LANES), lambda i: (0, 0)),
        grid=(1,),
        compiler_params=params(4),
        name="dots",
    )(got_two)
    dots = lax.all_to_all(dots_two, "row", split_axis=0, concat_axis=0, tiled=True)
    z = pl.pallas_call(
        gather_kernel,
        out_shape=field,
        in_specs=[smem_spec()] + [vmem_spec()] * 2,
        out_specs=vmem_spec(),
        compiler_params=params(8),
        cost_estimate=pl.CostEstimate(flops=10**8, bytes_accessed=2 * 10**6, transcendentals=0),
        name="gather",
    )(meta, fwd_two, got_two)
    return pl.pallas_call(
        finish_kernel,
        out_shape=(jax.ShapeDtypeStruct((LS, total), F32),) * 2,
        in_specs=[smem_spec()] + [vmem_spec()] * 4,
        out_specs=(vmem_spec(),) * 2,
        compiler_params=params(8),
        name="finish",
    )(noise_level, loc, w, z, dots)


def solution(mesh):
    placed = (P(None, ("row", "col")), P(("row", "col")), P(("row", "col")), P(), P(), P(), P())
    return jax.shard_map(
        on_device,
        mesh=mesh,
        in_specs=placed,
        out_specs=(P(None, ("row", "col")), P(None, ("row", "col"))),
        check_vma=False,
    )
```
